32 devices in a mesh: dp: 8 (over z, y), tensor: 4 (over x, core).
Axes of the slice: x: 2, y: 2, z: 4, core: 2. Of those that a mesh axis runs over, the one named last changes fastest.
Arguments:
- tokens: bfloat16 [32, 512, 1024], P('dp'), may hold values from -6 to 6
- cotangent: bfloat16 [32, 512, 1024], P('dp'), may hold values from -6 to 6
- live_count: int32 [8], P('dp'), may hold values from 1 to 4, as said below
- norm_first: float32 [1024], replicated, may hold values from 0.1 to 1.9
- w_query: bfloat16 [1024, 1024], P('dp', 'tensor'), may hold values from -0.1875 to 0.1875
- w_key: bfloat16 [1024, 1024], P('dp', 'tensor'), may hold values from -0.1875 to 0.1875
- w_value: bfloat16 [1024, 2048], P('dp', 'tensor'), may hold values from -0.1875 to 0.1875
- w_out_gate: bfloat16 [1024, 2048], P('dp', 'tensor'), may hold values from -0.1875 to 0.1875
- w_beta_decay: bfloat16 [1024, 2, 8], P('dp', None, 'tensor'), may hold values from -0.1875 to 0.1875
- conv_weight: float32 [4, 8, 512], replicated, may hold values from -3 to 3
- a_log: float32 [8], replicated, may hold values from 0 to 2
- dt_bias: float32 [8], replicated, may hold values from -6 to -2
- out_gain: float32 [256], replicated, may hold values from 0.1 to 1.9
- w_out: bfloat16 [2048, 1024], P('tensor', 'dp'), may hold values from -0.25 to 0.25
- norm_second: float32 [1024], replicated, may hold values from 0.1 to 1.9
- w_gate: bfloat16 [1024, 2816], P('dp', 'tensor'), may hold values from -0.1875 to 0.1875
- w_up: bfloat16 [1024, 2816], P('dp', 'tensor'), may hold values from -0.1875 to 0.1875
- w_down: bfloat16 [2816, 1024], P('tensor', 'dp'), may hold values from -0.21875 to 0.21875
Outputs:
- layer_out: bfloat16 [32, 512, 1024], P('dp')
- grad_tokens: float32 [32, 512, 1024], P('dp')
- grad_norm_first: float32 [1024], replicated
- grad_w_query: float32 [1024, 1024], P('dp', 'tensor')
- grad_w_key: float32 [1024, 1024], P('dp', 'tensor')
- grad_w_value: float32 [1024, 2048], P('dp', 'tensor')
- grad_w_out_gate: float32 [1024, 2048], P('dp', 'tensor')
- grad_w_beta_decay: float32 [1024, 2, 8], P('dp', None, 'tensor')
- grad_conv_weight: float32 [4, 8, 512], replicated
- grad_a_log: float32 [8], replicated
- grad_dt_bias: float32 [8], replicated
- grad_out_gain: float32 [256], replicated
- grad_w_out: float32 [2048, 1024], P('tensor', 'dp')
- grad_norm_second: float32 [1024], replicated
- grad_w_gate: float32 [1024, 2816], P('dp', 'tensor')
- grad_w_up: float32 [1024, 2816], P('dp', 'tensor')
- grad_w_down: float32 [2816, 1024], P('tensor', 'dp')
The draws below stay inside these ranges and needn't reach their ends.
Inputs may be any that keep to these rules, and one draw needn't show every extreme that they name: Slots 0 to live_count[i] - 1 of data device i hold sequences, the later ones padding outside the loss; some device has all 4 slots live.
All inputs are finite; a program needn't handle non-finite values.
Results may differ from the reference program's by a relative error of at most 0.022.
Values may be sent and summed in bfloat16 or wider, within the bound.
No kernel may reach another device: no remote copies, remote signals or barrier semaphores. Data moves between devices by JAX's collectives and lax.ppermute only.
A program may use at most 320 MiB of HBM per device.

```python
import jax
import jax.numpy as jnp
from jax import lax

D = 1024
H = 8
DK = 128
DV = 256
FF = 2816
KC = 4
BLOCK = 64
LEN = 512
SLOTS = 4
SEQS = 32
N_DP = 8
N_TENSOR = 4


def draw_live_count(key, part):
    key = jax.random.fold_in(key, 7)
    first_key, second_key = jax.random.split(key)
    devices = SEQS // SLOTS
    counts = jax.random.randint(first_key, (devices,), 1, SLOTS + 1)
    full_at = jax.random.randint(second_key, (), 0, devices)
    return counts.at[full_at].set(SLOTS).astype(jnp.int32)


def block_levels(key, shape, cuts, least, top_value):
    loudness = 1.0
    for position, parts in cuts:
        draws = jax.random.uniform(jax.random.fold_in(jax.random.fold_in(key, 6), position), (parts,), jnp.float32, least / len(cuts), top_value / len(cuts))
        loudness = loudness * jnp.repeat(jnp.exp(draws), shape[position] // parts).reshape((-1,) + (1,) * (len(shape) - 1 - position))
    return loudness


def scatter_about(key, shape, scale, reach, shards=(), held_as=jnp.bfloat16):
    factor_of = block_levels(key, shape, shards, -0.22, 0.18) if shards else 1.0
    array = jax.random.normal(key, shape, jnp.float32) * scale * factor_of
    return jnp.minimum(jnp.maximum(array, -reach), reach).astype(held_as)


def setup_inputs(seed: int = 0) -> dict:
    splits = jax.random.split(jax.random.key(seed), 19)
    tokens = scatter_about(splits[0], (SEQS, LEN, D), 1.0, 6.0, ((0, 8),))
    cotangent = scatter_about(splits[1], (SEQS, LEN, D), 1.0, 6.0, ((0, 8),))
    live_count = draw_live_count(jax.random.fold_in(splits[18], 71), 0)
    norm_first = jnp.clip(1.0 + 0.18 * jax.random.normal(splits[3], (D,), jnp.float32), 0.1, 1.9)
    w_query = scatter_about(splits[4], (D, H * DK), D ** -0.5, 0.1875, ((0, 8), (1, 4)))
    w_key = scatter_about(splits[5], (D, H * DK), D ** -0.5, 0.1875, ((0, 8), (1, 4)))
    w_value = scatter_about(splits[6], (D, H * DV), D ** -0.5, 0.1875, ((0, 8), (1, 4)))
    w_out_gate = scatter_about(splits[7], (D, H * DV), D ** -0.5, 0.1875, ((0, 8), (1, 4)))
    w_beta_decay = scatter_about(splits[8], (D, 2, H), D ** -0.5, 0.1875, ((0, 8), (2, 4)))
    conv_weight = scatter_about(splits[9], (KC, H, 2 * DK + DV), 0.5, 3.0, (), jnp.float32)
    a_log = jnp.clip(jax.random.uniform(splits[10], (H,), jnp.float32, 0.0, 2.0), 0.0, 2.0)
    dt_bias = jnp.clip(jax.random.uniform(splits[11], (H,), jnp.float32, -6.0, -2.0), -6.0, -2.0)
    out_gain = jnp.clip(1.0 + 0.18 * jax.random.normal(splits[12], (DV,), jnp.float32), 0.1, 1.9)
    w_out = scatter_about(splits[13], (H * DV, D), (H * DV // 4) ** -0.5, 0.25, ((0, 4), (1, 8)))
    norm_second = jnp.clip(1.0 + 0.18 * jax.random.normal(splits[14], (D,), jnp.float32), 0.1, 1.9)
    w_gate = scatter_about(splits[15], (D, FF), D ** -0.5, 0.1875, ((0, 8), (1, 4)))
    w_up = scatter_about(splits[16], (D, FF), D ** -0.5, 0.1875, ((0, 8), (1, 4)))
    w_down = scatter_about(splits[17], (FF, D), (FF // 4) ** -0.5, 0.21875, ((0, 4), (1, 8)))
    return dict(tokens=tokens, cotangent=cotangent, live_count=live_count, norm_first=norm_first, w_query=w_query, w_key=w_key, w_value=w_value, w_out_gate=w_out_gate, w_beta_decay=w_beta_decay, conv_weight=conv_weight, a_log=a_log, dt_bias=dt_bias, out_gain=out_gain, w_out=w_out, norm_second=norm_second, w_gate=w_gate, w_up=w_up, w_down=w_down)


EPS = 1e-06

@jax.custom_vjp
def low(v):
    return lax.optimization_barrier(v.astype(jnp.bfloat16)).astype(jnp.float32)

@jax.custom_vjp
def lowered_backward(v):
    return v

def low_keep(v):
    return (low(v), None)

def low_pass(kept, grad):
    return (grad,)

def back_keep(v):
    return (v, None)

def back_low(kept, grad):
    return (low(grad),)
low.defvjp(low_keep, low_pass)
lowered_backward.defvjp(back_keep, back_low)

def exact_precision(form, first_op, second_op):
    return jnp.einsum(form, first_op, second_op, precision=lax.Precision.HIGHEST)

def unit_rms(values_in):
    return values_in * lax.rsqrt(lax.optimization_barrier(jnp.mean(values_in * values_in, axis=-1, keepdims=True)) + EPS)

def unit_length(values_in):
    return values_in * lax.rsqrt(lax.optimization_barrier(jnp.sum(values_in * values_in, axis=-1, keepdims=True)) + EPS)

def causal_conv(signal, tap_weights):
    result = signal * tap_weights[0]
    for offset in range(1, tap_weights.shape[0]):
        moved = jnp.pad(signal, ((0, 0), (offset, 0), (0, 0)))[:, :signal.shape[1], :]
        result = result + moved * tap_weights[offset]
    return result

def delta_rule(queries, key_rows, values, write_rate, gate_log):
    block_len = queries.shape[2]
    positions = jnp.arange(block_len)
    lower_mask = (positions[:, None] >= positions[None, :]).astype(jnp.float32)
    strict = (positions[:, None] > positions[None, :]).astype(jnp.float32)
    cumulate = jnp.cumsum(gate_log, axis=-1)
    spread = jnp.where(lower_mask > 0, cumulate[..., :, None] - cumulate[..., None, :], 0.0)
    decay_mat = jnp.exp(spread) * lower_mask
    key_beta = key_rows * write_rate[..., None]
    inner_prod = exact_precision('bnik,bnjk->bnij', key_beta, key_rows)
    nilpotent = -(inner_prod * decay_mat * strict)
    inverse = jnp.eye(block_len, dtype=jnp.float32) + nilpotent
    power_mat = nilpotent
    for doubling in range(block_len.bit_length() - 2):
        power_mat = exact_precision('bnij,bnjk->bnik', power_mat, power_mat)
        inverse = inverse + exact_precision('bnij,bnjk->bnik', inverse, power_mat)
    exp_cum = jnp.exp(cumulate)
    fresh_base = exact_precision('bnij,bnjv->bniv', inverse, values * write_rate[..., None])
    key_weight = exact_precision('bnij,bnjk->bnik', inverse, key_beta * exp_cum[..., None])
    scores = exact_precision('bnik,bnjk->bnij', queries, key_rows) * decay_mat
    query_decay = queries * exp_cum[..., None]
    ending = cumulate[..., -1]
    key_decay = key_rows * jnp.exp(ending[..., None] - cumulate)[..., None]

    def block_step(memory, pieces):
        base_n, weight_n, score_n, query_n, keyd_n, end_n = pieces
        fresh_val = base_n - exact_precision('bck,bkv->bcv', weight_n, memory)
        result = exact_precision('bck,bkv->bcv', query_n, memory) + exact_precision('bcj,bjv->bcv', score_n, fresh_val)
        memory = memory * jnp.exp(end_n)[:, None, None] + exact_precision('bck,bcv->bkv', keyd_n, fresh_val)
        return (memory, result)
    batch_size = queries.shape[0]
    memory_zero = jnp.zeros((batch_size, queries.shape[3], values.shape[3]), jnp.float32)
    pieces = tuple((jnp.moveaxis(member, 1, 0) for member in (fresh_base, key_weight, scores, query_decay, key_decay, ending)))
    _, results = lax.scan(jax.checkpoint(block_step), memory_zero, pieces)
    return jnp.moveaxis(results, 0, 1)

def mix_heads(projected_rows, conv_part, log_rate, rate_shift, gain_part):
    seq_count, length, _ = projected_rows.shape
    tap_count, head_count, channels = conv_part.shape
    value_dim = gain_part.shape[0]
    key_dim = (channels - value_dim) // 2
    key_cols = head_count * key_dim
    value_cols = head_count * value_dim
    query_in = projected_rows[..., :key_cols]
    key_in = projected_rows[..., key_cols:2 * key_cols]
    value_in = projected_rows[..., 2 * key_cols:2 * key_cols + value_cols]
    gate_in = projected_rows[..., 2 * key_cols + value_cols:2 * key_cols + 2 * value_cols]
    write_in = projected_rows[..., 2 * key_cols + 2 * value_cols:2 * key_cols + 2 * value_cols + head_count]
    decay_in = projected_rows[..., 2 * key_cols + 2 * value_cols + head_count:]
    queries = unit_length(jax.nn.silu(causal_conv(query_in, conv_part[:, :, :key_dim].reshape(tap_count, key_cols))).reshape(seq_count, length, head_count, key_dim)) * key_dim ** (-0.5)
    key_rows = unit_length(jax.nn.silu(causal_conv(key_in, conv_part[:, :, key_dim:2 * key_dim].reshape(tap_count, key_cols))).reshape(seq_count, length, head_count, key_dim))
    values = jax.nn.silu(causal_conv(value_in, conv_part[:, :, 2 * key_dim:].reshape(tap_count, value_cols))).reshape(seq_count, length, head_count, value_dim)
    write_rate = jax.nn.sigmoid(write_in)
    gate_log = -jnp.exp(log_rate) * jax.nn.softplus(decay_in + rate_shift)
    blocks = length // BLOCK

    def arrange(member):
        member = jnp.moveaxis(member, 2, 1)
        return member.reshape((seq_count * head_count, blocks, BLOCK) + member.shape[3:])
    result = delta_rule(arrange(queries), arrange(key_rows), arrange(values), arrange(write_rate), arrange(gate_log))
    result = jnp.moveaxis(result.reshape(seq_count, head_count, length, value_dim), 1, 2)
    normed = unit_rms(result) * gain_part * jax.nn.silu(gate_in.reshape(seq_count, length, head_count, value_dim))
    return normed.reshape(seq_count, length, value_cols)

def layer_forward(tokens_in, params):
    norm_first, w_query, w_key, w_value, w_out_gate, w_beta_decay, conv_weight, a_log, dt_bias, out_gain, w_out, norm_second, w_gate, w_up, w_down = params
    groups = N_TENSOR
    head_count = H // groups
    ff_local = FF // groups
    input_normalized = low(unit_rms(tokens_in) * norm_first)
    widened_input = jnp.concatenate([w_query.reshape(D, groups, head_count * DK), w_key.reshape(D, groups, head_count * DK), w_value.reshape(D, groups, head_count * DV), w_out_gate.reshape(D, groups, head_count * DV), jnp.moveaxis(w_beta_decay.reshape(D, 2, groups, head_count), 2, 1).reshape(D, groups, 2 * head_count)], axis=2)
    projected_rows = lowered_backward(exact_precision('aeh,htu->taeu', input_normalized, widened_input))
    conv_groups = jnp.moveaxis(conv_weight.reshape(KC, groups, head_count, 2 * DK + DV), 1, 0)
    mixed_heads = jax.vmap(mix_heads, in_axes=(0, 0, 0, 0, None))(projected_rows, conv_groups, a_log.reshape(groups, head_count), dt_bias.reshape(groups, head_count), out_gain)
    partial_mix = exact_precision('jslc,jcd->jsld', low(mixed_heads), w_out.reshape(groups, head_count * DV, D))
    branch_mix = lowered_backward(lax.optimization_barrier(jnp.sum(low(partial_mix), axis=0)))
    hidden_res = tokens_in + branch_mix
    middle_normalized = low(unit_rms(hidden_res) * norm_second)
    paired_input = jnp.concatenate([w_gate.reshape(D, groups, ff_local), w_up.reshape(D, groups, ff_local)], axis=2)
    gate_up_product = lowered_backward(exact_precision('aeh,htu->taeu', middle_normalized, paired_input))
    activated = low(jax.nn.silu(gate_up_product[..., :ff_local]) * gate_up_product[..., ff_local:])
    partial_ff = exact_precision('jslf,jfd->jsld', activated, w_down.reshape(groups, ff_local, D))
    branch_ff = lowered_backward(lax.optimization_barrier(jnp.sum(low(partial_ff), axis=0)))
    return hidden_res + branch_ff

def reference(tokens, cotangent, live_count, norm_first, w_query, w_key, w_value, w_out_gate, w_beta_decay, conv_weight, a_log, dt_bias, out_gain, w_out, norm_second, w_gate, w_up, w_down):
    params = tuple((member.astype(jnp.float32) for member in (norm_first, w_query, w_key, w_value, w_out_gate, w_beta_decay, conv_weight, a_log, dt_bias, out_gain, w_out, norm_second, w_gate, w_up, w_down)))
    token_groups = tokens.reshape(N_DP, SLOTS, LEN, D)
    cot_groups = cotangent.reshape(N_DP, SLOTS, LEN, D)
    group_live = (jnp.arange(SLOTS)[None, :] < live_count[:, None]).astype(jnp.float32)
    zero_grads = jax.tree.map(jnp.zeros_like, params)

    def group_step(totals, member):
        group_tokens, group_cot, group_mask = member
        result, pull = jax.vjp(layer_forward, group_tokens.astype(jnp.float32), params)
        grad_x, grad_params = pull(group_cot.astype(jnp.float32) * group_mask[:, None, None])
        totals = jax.tree.map(lambda first_op, second_op: first_op + second_op, totals, grad_params)
        return (totals, (result.astype(jnp.bfloat16), grad_x))
    grads, (outputs, grad_x) = lax.scan(group_step, zero_grads, (token_groups, cot_groups, group_live))
    return (outputs.reshape(SEQS, LEN, D), grad_x.reshape(SEQS, LEN, D), grads[0], grads[1], grads[2], grads[3], grads[4], grads[5], grads[6], grads[7], grads[8], grads[9], grads[10], grads[11], grads[12], grads[13], grads[14])
```

```python
import functools

import jax
import jax.numpy as jnp
from jax import lax
from jax.experimental import pallas as pl
from jax.experimental.layout import Layout, with_layout_constraint
from jax.experimental.pallas import tpu as pltpu
from jax.sharding import PartitionSpec as P

BLOCK = 64


EPS = 1e-06


def exact_precision(form, first_op, second_op):
    return jnp.einsum(form, first_op, second_op, precision=lax.Precision.HIGHEST)


def unit_rms(values_in):
    return values_in * lax.rsqrt(jnp.mean(values_in * values_in, axis=-1, keepdims=True) + EPS)


def unit_length(values_in):
    return values_in * lax.rsqrt(jnp.sum(values_in * values_in, axis=-1, keepdims=True) + EPS)


def causal_conv(signal, tap_weights):
    result = signal * tap_weights[0]
    for offset in range(1, tap_weights.shape[0]):
        moved = jnp.pad(signal, ((0, 0), (offset, 0), (0, 0)))[:, : signal.shape[1], :]
        result = result + moved * tap_weights[offset]
    return result


def delta_rule(queries, key_rows, values, write_rate, gate_log):
    block_len = queries.shape[2]
    positions = jnp.arange(block_len)
    lower_mask = (positions[:, None] >= positions[None, :]).astype(jnp.float32)
    strict = (positions[:, None] > positions[None, :]).astype(jnp.float32)
    cumulate = jnp.cumsum(gate_log, axis=-1)
    spread = jnp.where(lower_mask > 0, cumulate[..., :, None] - cumulate[..., None, :], 0.0)
    decay_mat = jnp.exp(spread) * lower_mask
    key_beta = key_rows * write_rate[..., None]
    inner_prod = exact_precision("bnik,bnjk->bnij", key_beta, key_rows)
    nilpotent = -(inner_prod * decay_mat * strict)
    inverse = jnp.eye(block_len, dtype=jnp.float32) + nilpotent
    power_mat = nilpotent
    for doubling in range(block_len.bit_length() - 2):
        power_mat = exact_precision("bnij,bnjk->bnik", power_mat, power_mat)
        inverse = inverse + exact_precision("bnij,bnjk->bnik", inverse, power_mat)
    exp_cum = jnp.exp(cumulate)
    fresh_base = exact_precision("bnij,bnjv->bniv", inverse, values * write_rate[..., None])
    key_weight = exact_precision("bnij,bnjk->bnik", inverse, key_beta * exp_cum[..., None])
    scores = exact_precision("bnik,bnjk->bnij", queries, key_rows) * decay_mat
    query_decay = queries * exp_cum[..., None]
    ending = cumulate[..., -1]
    key_decay = key_rows * jnp.exp(ending[..., None] - cumulate)[..., None]

    def block_step(memory, pieces):
        base_n, weight_n, score_n, query_n, keyd_n, end_n = pieces
        fresh_val = base_n - exact_precision("bck,bkv->bcv", weight_n, memory)
        result = exact_precision("bck,bkv->bcv", query_n, memory) + exact_precision(
            "bcj,bjv->bcv", score_n, fresh_val
        )
        memory = memory * jnp.exp(end_n)[:, None, None] + exact_precision(
            "bck,bcv->bkv", keyd_n, fresh_val
        )
        return (memory, result)

    batch_size = queries.shape[0]
    memory_zero = jnp.zeros((batch_size, queries.shape[3], values.shape[3]), jnp.float32)
    pieces = tuple(
        (
            jnp.moveaxis(member, 1, 0)
            for member in (fresh_base, key_weight, scores, query_decay, key_decay, ending)
        )
    )
    _, results = lax.scan(jax.checkpoint(block_step), memory_zero, pieces)
    return jnp.moveaxis(results, 0, 1)


def mix_heads(projected_rows, conv_part, log_rate, rate_shift, gain_part):
    seq_count, length, _ = projected_rows.shape
    tap_count, head_count, channels = conv_part.shape
    value_dim = gain_part.shape[0]
    key_dim = (channels - value_dim) // 2
    key_cols = head_count * key_dim
    value_cols = head_count * value_dim
    query_in = projected_rows[..., :key_cols]
    key_in = projected_rows[..., key_cols : 2 * key_cols]
    value_in = projected_rows[..., 2 * key_cols : 2 * key_cols + value_cols]
    gate_in = projected_rows[..., 2 * key_cols + value_cols : 2 * key_cols + 2 * value_cols]
    write_in = projected_rows[
        ..., 2 * key_cols + 2 * value_cols : 2 * key_cols + 2 * value_cols + head_count
    ]
    decay_in = projected_rows[..., 2 * key_cols + 2 * value_cols + head_count :]
    queries = unit_length(
        jax.nn.silu(
            causal_conv(query_in, conv_part[:, :, :key_dim].reshape(tap_count, key_cols))
        ).reshape(seq_count, length, head_count, key_dim)
    ) * key_dim ** (-0.5)
    key_rows = unit_length(
        jax.nn.silu(
            causal_conv(key_in, conv_part[:, :, key_dim : 2 * key_dim].reshape(tap_count, key_cols))
        ).reshape(seq_count, length, head_count, key_dim)
    )
    values = jax.nn.silu(
        causal_conv(value_in, conv_part[:, :, 2 * key_dim :].reshape(tap_count, value_cols))
    ).reshape(seq_count, length, head_count, value_dim)
    write_rate = jax.nn.sigmoid(write_in)
    gate_log = -jnp.exp(log_rate) * jax.nn.softplus(decay_in + rate_shift)
    blocks = length // BLOCK

    def arrange(member):
        member = jnp.moveaxis(member, 2, 1)
        return member.reshape((seq_count * head_count, blocks, BLOCK) + member.shape[3:])

    result = delta_rule(
        arrange(queries), arrange(key_rows), arrange(values), arrange(write_rate), arrange(gate_log)
    )
    result = jnp.moveaxis(result.reshape(seq_count, head_count, length, value_dim), 1, 2)
    normed = (
        unit_rms(result)
        * gain_part
        * jax.nn.silu(gate_in.reshape(seq_count, length, head_count, value_dim))
    )
    return normed.reshape(seq_count, length, value_cols)


def outer_dot(first_op, second_op):
    return lax.dot_general(
        first_op, second_op, (((0,), (0,)), ((), ())), preferred_element_type=jnp.float32
    )


def inner_dot(first_op, second_op):
    return lax.dot_general(
        first_op, second_op, (((1,), (1,)), ((), ())), preferred_element_type=jnp.float32
    )


def rms_back(values_in, cotan):
    return jax.vjp(unit_rms, values_in)[1](cotan)[0]


def gather_first(shards):
    return (
        lax.all_gather(shards[0], "dp", axis=0, tiled=True),
        lax.all_gather(shards[1], "dp", axis=0, tiled=True),
        lax.all_gather(shards[2], "dp", axis=0, tiled=True),
        lax.all_gather(shards[3], "dp", axis=0, tiled=True),
        lax.all_gather(shards[4], "dp", axis=0, tiled=True),
        lax.all_gather(shards[5], "dp", axis=1, tiled=True),
        lax.all_gather(shards[6], "dp", axis=0, tiled=True),
        lax.all_gather(shards[7], "dp", axis=0, tiled=True),
        lax.all_gather(shards[8], "dp", axis=1, tiled=True),
    )


def gather_again(shards):
    return (
        lax.all_gather(shards[0], "dp", axis=0, tiled=True),
        lax.all_gather(shards[1], "dp", axis=0, tiled=True),
        lax.all_gather(shards[2], "dp", axis=0, tiled=True),
        lax.all_gather(shards[3], "dp", axis=0, tiled=True),
        lax.all_gather(shards[4], "dp", axis=0, tiled=True),
        lax.all_gather(shards[5], "dp", axis=1, tiled=True),
        lax.all_gather(shards[6], "dp", axis=0, tiled=True),
        lax.all_gather(shards[7], "dp", axis=0, tiled=True),
        lax.all_gather(shards[8], "dp", axis=1, tiled=True),
    )


def branch_sum(partial_rows):
    return lax.psum(partial_rows.astype(jnp.bfloat16), "tensor").astype(jnp.float32)


def grad_sum(partial_rows):
    return lax.psum(partial_rows.astype(jnp.bfloat16), "tensor").astype(jnp.float32)


def assemble(gathered, model_width):
    (
        full_query,
        full_key,
        full_value,
        full_gate_out,
        full_beta_decay,
        full_out,
        full_gate,
        full_up,
        full_down,
    ) = gathered
    widened_input = jnp.concatenate(
        [full_query, full_key, full_value, full_gate_out, full_beta_decay.reshape(model_width, -1)],
        axis=1,
    )
    paired_input = jnp.concatenate([full_gate, full_up], axis=1)
    return (widened_input, paired_input, full_out, full_down)


LOW = jnp.bfloat16
WIDE = jnp.float32
VMEM_BYTES = 58 * 1024 * 1024


def mxu(first_op, second_op, first_dim=1, second_dim=0):
    return lax.dot_general(
        first_op.astype(LOW),
        second_op.astype(LOW),
        (((first_dim,), (second_dim,)), ((), ())),
        preferred_element_type=WIDE,
    )


def mxu_split(first_op, second_op):
    first_high = first_op.astype(LOW)
    first_rest = (first_op - first_high.astype(WIDE)).astype(LOW)
    second_high = second_op.astype(LOW)
    second_rest = (second_op - second_high.astype(WIDE)).astype(LOW)
    return (
        mxu(first_high, second_high)
        + mxu(first_high, second_rest)
        + mxu(first_rest, second_high)
    )


def move_down(signal, offset):
    if offset == 0:
        return signal
    row = lax.broadcasted_iota(jnp.int32, signal.shape, 0)
    return jnp.where(row >= offset, pltpu.roll(signal, offset, 0), 0.0)


def move_up(signal, offset):
    if offset == 0:
        return signal
    length = signal.shape[0]
    row = lax.broadcasted_iota(jnp.int32, signal.shape, 0)
    return jnp.where(row < length - offset, pltpu.roll(signal, length - offset, 0), 0.0)


def conv_rows(signal, taps):
    result = signal * taps[0:1]
    for offset in range(1, taps.shape[0]):
        result = result + move_down(signal, offset) * taps[offset : offset + 1]
    return result


def conv_back(grad, signal, taps):
    result = grad * taps[0:1]
    for offset in range(1, taps.shape[0]):
        result = result + move_up(grad, offset) * taps[offset : offset + 1]
    tap_grads = [
        jnp.sum(grad * move_down(signal, offset), axis=0, keepdims=True)
        for offset in range(taps.shape[0])
    ]
    return result, tap_grads


def silu_back(values_in, sig):
    return sig * (1.0 + values_in * (1.0 - sig))


def block_masks(size):
    row = lax.broadcasted_iota(jnp.int32, (size, size), 0)
    col = lax.broadcasted_iota(jnp.int32, (size, size), 1)
    same = (row // BLOCK) == (col // BLOCK)
    return same & (row >= col), same & (row > col), row == col


def decay_of(lower, cum_col, cum_row):
    return jnp.where(lower, jnp.exp(jnp.where(lower, cum_col - cum_row, 0.0)), 0.0)


def unit_inverse(strict_part, eye):
    inverse = eye - strict_part
    power = -strict_part
    for _ in range(BLOCK.bit_length() - 2):
        power = mxu(power, power)
        inverse = inverse + mxu(inverse, power)
    rest = eye - inverse - mxu_split(strict_part, inverse)
    return inverse + mxu(inverse, rest)


class Sizes:
    def __init__(self, length, heads, key_dim, value_dim):
        self.length, self.heads, self.key_dim, self.value_dim = length, heads, key_dim, value_dim
        self.stack = min(256, length)
        self.stacks = length // self.stack
        self.chunks = length // BLOCK
        self.per_stack = self.stack // BLOCK
        self.conv_cols = heads * (2 * key_dim + value_dim)
        self.cols = self.conv_cols + heads * value_dim

    def parts(self, head):
        k, v, n = self.key_dim, self.value_dim, self.heads
        return (
            slice(head * k, (head + 1) * k),
            slice((n + head) * k, (n + head + 1) * k),
            slice(2 * n * k + head * v, 2 * n * k + (head + 1) * v),
            slice(2 * n * k + (n + head) * v, 2 * n * k + (n + head + 1) * v),
        )


def head_inputs(sz, proj_ref, taps_ref, head):
    q_at, k_at, v_at, _ = sz.parts(head)
    kept = []
    for at in (q_at, k_at, v_at):
        raw = proj_ref[0, :, at]
        taps = taps_ref[0, :, at]
        mixed = conv_rows(raw, taps)
        sig = jax.nn.sigmoid(mixed)
        kept.append((raw, taps, mixed, sig, mixed * sig))
    q_inv = lax.rsqrt(jnp.sum(kept[0][4] * kept[0][4], axis=-1, keepdims=True) + EPS)
    k_inv = lax.rsqrt(jnp.sum(kept[1][4] * kept[1][4], axis=-1, keepdims=True) + EPS)
    q_unit = kept[0][4] * q_inv
    keys = kept[1][4] * k_inv
    return kept, q_inv, k_inv, q_unit, keys, kept[2][4]


def forward_kernel(sz, x_ref, w_ref, taps_ref, col_ref, row_ref, gain_ref,
                   proj_ref, mixed_ref, o_ref, fresh_ref, state_ref, inv_ref):
    n = sz.heads
    depth = x_ref.shape[1]
    proj_ref[0] = mxu(x_ref[...], w_ref[0].reshape(depth, sz.cols))
    lower, strict, diag = block_masks(sz.stack)
    eye = diag.astype(WIDE)
    held = []
    for head in range(n):
        _, _, _, q_unit, keys, values = head_inputs(sz, proj_ref, taps_ref, head)
        queries = q_unit * (sz.key_dim ** -0.5)
        beta = col_ref[0, :, head : head + 1]
        cum = col_ref[0, :, n + head : n + head + 1]
        tail = col_ref[0, :, 2 * n + head : 2 * n + head + 1]
        q_low, k_low = queries.astype(LOW), keys.astype(LOW)
        scores, inverses = [], []
        for s in range(sz.stacks):
            at = slice(s * sz.stack, (s + 1) * sz.stack)
            decay = decay_of(lower, cum[at], row_ref[0, head : head + 1, at])
            inner = mxu(k_low[at], k_low[at], 1, 1) * decay * beta[at]
            inverse = unit_inverse(jnp.where(strict, inner, 0.0), eye)
            inv_ref[0, head, s] = inverse.astype(LOW)
            inverses.append(inverse.astype(LOW))
            scores.append((mxu(q_low[at], k_low[at], 1, 1) * decay).astype(LOW))
        exp_cum = jnp.exp(cum)
        key_tail = (keys * jnp.exp(tail)).astype(LOW)
        held.append((q_low, k_low, values, beta, cum, exp_cum, key_tail, scores, inverses))
    memory = [jnp.zeros((sz.key_dim, sz.value_dim), WIDE) for _ in range(n)]
    from_state = [[] for _ in range(n)]
    fresh = [[] for _ in range(n)]
    for c in range(sz.chunks):
        at = slice(c * BLOCK, (c + 1) * BLOCK)
        inner_at = slice((c % sz.per_stack) * BLOCK, (c % sz.per_stack + 1) * BLOCK)
        for head in range(n):
            q_low, k_low, values, beta, cum, exp_cum, key_tail, scores, inverses = held[head]
            memory_low = memory[head].astype(LOW)
            state_ref[0, head, c] = memory_low
            both = mxu(jnp.concatenate([k_low[at], q_low[at]], axis=0), memory_low)
            right = beta[at] * (values[at] - exp_cum[at] * both[:BLOCK])
            solved = mxu(inverses[c // sz.per_stack][inner_at, inner_at], right).astype(LOW)
            from_state[head].append(exp_cum[at] * both[BLOCK:])
            fresh[head].append(solved)
            last = slice((c + 1) * BLOCK - 1, (c + 1) * BLOCK)
            memory[head] = memory[head] * jnp.exp(cum[last]) + mxu(key_tail[at], solved, 0, 0)
    gain = gain_ref[...]
    for head in range(n):
        gate_at = sz.parts(head)[3]
        v_at = slice(head * sz.value_dim, (head + 1) * sz.value_dim)
        scores = held[head][7]
        for s in range(sz.stacks):
            at = slice(s * sz.stack, (s + 1) * sz.stack)
            of = slice(s * sz.per_stack, (s + 1) * sz.per_stack)
            solved = jnp.concatenate(fresh[head][of], axis=0)
            result = jnp.concatenate(from_state[head][of], axis=0) + mxu(scores[s], solved)
            fresh_ref[0, at, v_at] = solved
            o_ref[0, at, v_at] = result
            gate = proj_ref[0, at, gate_at]
            inv = lax.rsqrt(jnp.mean(result * result, axis=-1, keepdims=True) + EPS)
            mixed_ref[0, at, v_at] = (
                result * inv * gain * (gate * jax.nn.sigmoid(gate))
            ).astype(LOW)


def out_rows(wo_ref, count):
    return jnp.concatenate([wo_ref[0, i, :count] for i in range(wo_ref.shape[1])], axis=1)


def backward_kernel(sz, rank_ref, xt_ref, w_ref, wo_ref, gb_ref, gbt_ref, taps_ref, col_ref, row_ref,
                    gain_ref, proj_ref, mixed_ref, o_ref, fresh_ref, state_ref, inv_ref,
                    ga_ref, gb_out_ref, gin_ref, gcol_ref, grow_ref, gend_ref, gtaps_ref, ggain_ref,
                    gp_ref):
    n = sz.heads
    depth = xt_ref.shape[0]
    wo = out_rows(wo_ref, n * sz.value_dim)
    gate_cols = sz.cols - sz.conv_cols
    row_shape = ga_ref.shape[1:3]
    gb_out_ref[0, :, :, gate_cols:] = (
        mxu(gbt_ref[...], mixed_ref[0]).astype(LOW).reshape(row_shape + (gate_cols,))
    )
    grad_heads = mxu(gb_ref[...], wo, 1, 1)
    lower, strict, _ = block_masks(sz.stack)
    gain = gain_ref[...]
    step = pl.program_id(0)

    @pl.when(step == 0)
    def _():
        ggain_ref[...] = jnp.zeros_like(ggain_ref)
        gin_ref[...] = jnp.zeros_like(gin_ref)

    held = []
    for head in range(n):
        kept, q_inv, k_inv, q_unit, keys, values = head_inputs(sz, proj_ref, taps_ref, head)
        queries = q_unit * (sz.key_dim ** -0.5)
        v_at = slice(head * sz.value_dim, (head + 1) * sz.value_dim)
        gate_at = sz.parts(head)[3]
        gate = proj_ref[0, :, gate_at]
        sig = jax.nn.sigmoid(gate)
        result = o_ref[0, :, v_at]
        inv = lax.rsqrt(jnp.mean(result * result, axis=-1, keepdims=True) + EPS)
        unit = result * inv
        d_head = grad_heads[:, v_at]
        d_unit_gate = d_head * unit
        ggain_ref[...] += jnp.sum(d_unit_gate * (gate * sig), axis=0, keepdims=True)
        gp_ref[:, gate_at] = (d_unit_gate * gain * silu_back(gate, sig)).astype(LOW)
        d_unit = d_head * gain * (gate * sig)
        d_o = inv * (d_unit - unit * jnp.mean(d_unit * unit, axis=-1, keepdims=True))
        beta = col_ref[0, :, head : head + 1]
        cum = col_ref[0, :, n + head : n + head + 1]
        tail = col_ref[0, :, 2 * n + head : 2 * n + head + 1]
        q_low, k_low, do_low = queries.astype(LOW), keys.astype(LOW), d_o.astype(LOW)
        exp_cum, exp_tail = jnp.exp(cum), jnp.exp(tail)
        key_tail = keys * exp_tail
        decays, inners, scores, through = [], [], [], []
        for s in range(sz.stacks):
            at = slice(s * sz.stack, (s + 1) * sz.stack)
            decay = decay_of(lower, cum[at], row_ref[0, head : head + 1, at])
            score = mxu(q_low[at], k_low[at], 1, 1) * decay
            inners.append(jnp.where(strict, mxu(k_low[at], k_low[at], 1, 1) * decay, 0.0))
            decays.append(decay)
            scores.append(score)
            through.append(mxu(score, do_low[at], 0, 0))
        held.append(dict(
            kept=kept, q_inv=q_inv, k_inv=k_inv, q_unit=q_unit, keys=keys, values=values,
            d_o=d_o, do_low=do_low, beta=beta, cum=cum, q_low=q_low, k_low=k_low,
            exp_cum=exp_cum, exp_tail=exp_tail, key_tail=key_tail, decays=decays,
            inners=inners, scores=scores, through=through,
            d_right=[None] * sz.chunks, d_q=[None] * sz.chunks, d_k=[None] * sz.chunks,
            d_beta=[None] * sz.chunks, d_cum=[None] * sz.chunks, x=[None] * sz.chunks,
            d_v=[None] * sz.chunks,
        ))
    d_memory = [jnp.zeros((sz.key_dim, sz.value_dim), WIDE) for _ in range(n)]
    for c in reversed(range(sz.chunks)):
        at = slice(c * BLOCK, (c + 1) * BLOCK)
        s, local = c // sz.per_stack, c % sz.per_stack
        in_at = slice(local * BLOCK, (local + 1) * BLOCK)
        for head in range(n):
            m = held[head]
            v_at = slice(head * sz.value_dim, (head + 1) * sz.value_dim)
            memory_low = state_ref[0, head, c]
            grad_low = d_memory[head].astype(LOW)
            d_fresh = m["through"][s][in_at] + mxu(m["key_tail"][at], grad_low)
            d_right = mxu(inv_ref[0, head, s, in_at, in_at], d_fresh, 0, 0)
            d_z = m["beta"][at] * d_right
            lifted = m["exp_cum"][at] * m["d_o"][at]
            sunk = -m["exp_cum"][at] * d_z
            pair = jnp.concatenate([lifted.astype(LOW), sunk.astype(LOW)], axis=0)
            rows = jnp.concatenate([m["q_low"][at], m["k_low"][at]], axis=0)
            last = jnp.exp(m["cum"][(c + 1) * BLOCK - 1 : (c + 1) * BLOCK])
            gend_ref[0, head, c : c + 1, :] = last * jnp.sum(
                d_memory[head] * memory_low.astype(WIDE), axis=0, keepdims=True
            )
            d_tail = mxu(fresh_ref[0, at, v_at], grad_low, 1, 1)
            d_memory[head] = d_memory[head] * last + mxu(rows, pair, 0, 0)
            back = mxu(pair, memory_low, 1, 1)
            both = mxu(rows, memory_low)
            from_keys = m["exp_cum"][at] * both[BLOCK:]
            x = jnp.sum(d_tail * m["key_tail"][at], axis=-1, keepdims=True)
            m["x"][c] = x
            m["d_right"][c] = d_right
            m["d_v"][c] = d_z
            m["d_q"][c] = back[:BLOCK]
            m["d_k"][c] = back[BLOCK:] + d_tail * m["exp_tail"][at]
            m["d_beta"][c] = jnp.sum(
                d_right * (m["values"][at] - from_keys), axis=-1, keepdims=True
            )
            m["d_cum"][c] = (
                jnp.sum(lifted * both[:BLOCK], axis=-1, keepdims=True)
                - jnp.sum(d_z * from_keys, axis=-1, keepdims=True)
                - x
            )
    lane = lax.broadcasted_iota(jnp.int32, (sz.stack, gcol_ref.shape[2]), 1)
    columns = [jnp.zeros((sz.stack, gcol_ref.shape[2]), WIDE) for _ in range(sz.stacks)]
    for head in range(n):
        m = held[head]
        q_at, k_at, v_at, _ = sz.parts(head)
        own = slice(head * sz.value_dim, (head + 1) * sz.value_dim)
        d_q, d_k = [], []
        for s in range(sz.stacks):
            at = slice(s * sz.stack, (s + 1) * sz.stack)
            of = slice(s * sz.per_stack, (s + 1) * sz.per_stack)
            solved = fresh_ref[0, at, own]
            d_right = jnp.concatenate(m["d_right"][of], axis=0)
            d_score = mxu(m["do_low"][at], solved, 1, 1)
            d_inner = -jnp.where(strict, mxu(d_right, solved, 1, 1), 0.0)
            decay, inner, beta = m["decays"][s], m["inners"][s], m["beta"][at]
            d_qk = d_score * decay
            d_kk = d_inner * decay * beta
            by_beta = d_inner * inner
            spread = d_score * m["scores"][s] + by_beta * beta
            d_q.append(jnp.concatenate(m["d_q"][of], axis=0) + mxu(d_qk, m["k_low"][at]))
            d_k.append(
                jnp.concatenate(m["d_k"][of], axis=0)
                + mxu(d_qk, m["q_low"][at], 0, 0)
                + mxu(d_kk, m["k_low"][at], 0, 0)
                + mxu(d_kk, m["k_low"][at])
            )
            grow_ref[0, head : head + 1, at] = jnp.sum(spread, axis=0, keepdims=True)
            d_beta = jnp.concatenate(m["d_beta"][of], axis=0) + jnp.sum(
                by_beta, axis=-1, keepdims=True
            )
            d_cum = jnp.concatenate(m["d_cum"][of], axis=0) + jnp.sum(
                spread, axis=-1, keepdims=True
            )
            x = jnp.concatenate(m["x"][of], axis=0)
            columns[s] = jnp.where(lane == head, d_beta, columns[s])
            columns[s] = jnp.where(lane == n + head, d_cum, columns[s])
            columns[s] = jnp.where(lane == 2 * n + head, x, columns[s])
        d_q = jnp.concatenate(d_q, axis=0)
        d_k = jnp.concatenate(d_k, axis=0)
        d_v = jnp.concatenate(m["d_v"], axis=0)
        q_unit, keys = m["q_unit"], m["keys"]
        d_qs = (sz.key_dim ** -0.5) * m["q_inv"] * (
            d_q - q_unit * jnp.sum(d_q * q_unit, axis=-1, keepdims=True)
        )
        d_ks = m["k_inv"] * (d_k - keys * jnp.sum(d_k * keys, axis=-1, keepdims=True))
        for at, grad, (raw, taps, mixed, sig, _) in zip(
            (q_at, k_at, v_at), (d_qs, d_ks, d_v), m["kept"]
        ):
            d_raw, d_taps = conv_back(grad * silu_back(mixed, sig), raw, taps)
            gp_ref[:, at] = d_raw.astype(LOW)
            for j, member in enumerate(d_taps):
                gtaps_ref[0, j : j + 1, at] = member
    for s in range(sz.stacks):
        gcol_ref[0, s * sz.stack : (s + 1) * sz.stack] = columns[s]
    ga_ref[0] = mxu(xt_ref[...], gp_ref[:, : sz.conv_cols]).astype(LOW).reshape(ga_ref.shape[1:])
    gb_out_ref[0, :, :, :gate_cols] = (
        mxu(xt_ref[...], gp_ref[:, sz.conv_cols :]).astype(LOW).reshape(row_shape + (gate_cols,))
    )
    gin_ref[...] += mxu(gp_ref[...], w_ref[0].reshape(depth, sz.cols), 1, 1)


def out_kernel(mixed_ref, wo_ref, acc_ref):
    @pl.when(pl.program_id(0) == 0)
    def _():
        acc_ref[...] = jnp.zeros_like(acc_ref)

    acc_ref[...] += mxu(mixed_ref[0], out_rows(wo_ref, mixed_ref.shape[2]))


def feed_kernel(n_ref, g_ref, w_ref, out_ref, gmid_ref, gw_ref):
    @pl.when(pl.program_id(0) == 0)
    def _():
        out_ref[...] = jnp.zeros_like(out_ref)
        gmid_ref[...] = jnp.zeros_like(gmid_ref)

    owners, _, width, share = w_ref.shape[1:]

    def weight(which):
        return jnp.concatenate([w_ref[0, i, which] for i in range(owners)], axis=1)

    def keep(which, value):
        value = value.astype(LOW)
        for i in range(owners):
            gw_ref[0, i, which] = value[:, i * share : (i + 1) * share]

    rows, grads = n_ref[...], g_ref[...]
    w_gate, w_up, w_down = weight(0), weight(1), weight(2)
    gate = mxu(rows, w_gate, 1, 1)
    up = mxu(rows, w_up, 1, 1)
    sig = jax.nn.sigmoid(gate)
    act = (gate * sig * up).astype(LOW)
    out_ref[...] += mxu(act, w_down)
    d_act = mxu(grads, w_down, 1, 1)
    d_gate = (d_act * up * silu_back(gate, sig)).astype(LOW)
    d_up = (d_act * (gate * sig)).astype(LOW)
    gmid_ref[...] += mxu(d_gate, w_gate) + mxu(d_up, w_up)
    keep(0, mxu(d_gate, rows, 0, 0))
    keep(1, mxu(d_up, rows, 0, 0))
    keep(2, mxu(act, grads, 0, 0))


def grouped_call(kernel, steps, inputs, outputs, scratch=(), rank=None, group_of=None, flops=1):
    def spec(shape, by_group, buffers, place):
        rest = (0,) * (len(shape) - 1)
        if by_group:
            return pl.BlockSpec(
                (1,) + tuple(shape[1:]),
                lambda s, *r: (place(s, *r),) + rest,
                pipeline_mode=pl.Buffered(buffers),
            )
        return pl.BlockSpec(tuple(shape), lambda s, *r: (0,) + rest)

    def in_step(s, *r):
        return s

    in_place = in_step if group_of is None else lambda s, r: group_of(s, r[0])
    prefetch = () if rank is None else (rank,)
    return pl.pallas_call(
        kernel,
        grid_spec=pltpu.PrefetchScalarGridSpec(
            num_scalar_prefetch=len(prefetch),
            grid=(steps,),
            in_specs=[spec(a.shape, b > 0, b, in_place) for a, b in inputs],
            out_specs=[spec(s, by_group, 2, in_step) for s, _, by_group in outputs],
            scratch_shapes=list(scratch),
        ),
        out_shape=[jax.ShapeDtypeStruct(s, d) for s, d, _ in outputs],
        compiler_params=pltpu.CompilerParams(
            vmem_limit_bytes=VMEM_BYTES, dimension_semantics=("arbitrary",)
        ),
        cost_estimate=pl.CostEstimate(flops=flops, bytes_accessed=1, transcendentals=0),
    )(*prefetch, *[a for a, _ in inputs])


def body(
    tokens,
    cotangent,
    live_count,
    norm_first,
    w_query,
    w_key,
    w_value,
    w_out_gate,
    w_beta_decay,
    conv_weight,
    a_log,
    dt_bias,
    out_gain,
    w_out,
    norm_second,
    w_gate,
    w_up,
    w_down,
):
    slot_count, length, model_width = tokens.shape
    total_rows = slot_count * length
    head_count = a_log.shape[0] // lax.axis_size("tensor")
    head_start = lax.axis_index("tensor") * head_count
    conv_local = lax.dynamic_slice_in_dim(conv_weight, head_start, head_count, 1)
    decay_scale = lax.dynamic_slice_in_dim(a_log, head_start, head_count, 0)
    decay_shift = lax.dynamic_slice_in_dim(dt_bias, head_start, head_count, 0)
    shards = (w_query, w_key, w_value, w_out_gate, w_beta_decay, w_out, w_gate, w_up, w_down)
    widened_input, paired_input, out_proj, down_proj = assemble(gather_first(shards), model_width)
    tokens_in = tokens.reshape(total_rows, model_width).astype(jnp.float32)
    scaled_in = unit_rms(tokens_in)
    input_normalized = (scaled_in * norm_first).astype(jnp.bfloat16)
    projected_rows = jnp.dot(input_normalized, widened_input, preferred_element_type=jnp.float32)

    def mix_flat(proj_flat, conv_part, scale_part, shift_part, gain_part):
        return mix_heads(
            proj_flat.reshape(slot_count, length, -1), conv_part, scale_part, shift_part, gain_part
        ).reshape(total_rows, -1)

    mixed_heads, mix_pull = jax.vjp(
        mix_flat, projected_rows, conv_local, decay_scale, decay_shift, out_gain
    )
    mixed_low = mixed_heads.astype(jnp.bfloat16)
    hidden_res = tokens_in + branch_sum(
        jnp.dot(mixed_low, out_proj, preferred_element_type=jnp.float32)
    )
    scaled_mid = unit_rms(hidden_res)
    middle_normalized = (scaled_mid * norm_second).astype(jnp.bfloat16)
    gate_up_product = jnp.dot(middle_normalized, paired_input, preferred_element_type=jnp.float32)
    ff_local = paired_input.shape[1] // 2
    gate_part = gate_up_product[:, :ff_local]
    up_part = gate_up_product[:, ff_local:]
    sigmoid_gate = jax.nn.sigmoid(gate_part)
    silu_gate = gate_part * sigmoid_gate
    activated = (silu_gate * up_part).astype(jnp.bfloat16)
    result_rows = hidden_res + branch_sum(
        jnp.dot(activated, down_proj, preferred_element_type=jnp.float32)
    )
    layer_out = result_rows.astype(jnp.bfloat16).reshape(tokens.shape)
    live_rows = (jnp.arange(slot_count) < live_count[0]).astype(jnp.float32)
    grad_rows = (cotangent.astype(jnp.float32) * live_rows[:, None, None]).reshape(
        total_rows, model_width
    )
    back_wide, back_pair, back_out, back_down = assemble(gather_again(shards), model_width)
    grad_low = grad_rows.astype(jnp.bfloat16)
    grad_down_w = outer_dot(activated, grad_low)
    grad_act = inner_dot(grad_low, back_down)
    grad_gate = grad_act * up_part * sigmoid_gate * (1.0 + gate_part * (1.0 - sigmoid_gate))
    grad_up = grad_act * silu_gate
    grad_pair = jnp.concatenate([grad_gate, grad_up], axis=1).astype(jnp.bfloat16)
    grad_pair_w = outer_dot(middle_normalized, grad_pair)
    grad_mid_part = inner_dot(grad_pair, back_pair)
    gain_mid = jnp.sum(grad_mid_part * scaled_mid, axis=0)
    grad_mid = grad_sum(grad_mid_part)
    grad_hidden = grad_rows + rms_back(hidden_res, grad_mid * norm_second)
    grad_hidden_low = grad_hidden.astype(jnp.bfloat16)
    grad_out_w = outer_dot(mixed_low, grad_hidden_low)
    grad_heads = inner_dot(grad_hidden_low, back_out)
    grad_proj, grad_conv, grad_scale, grad_shift, grad_gain = mix_pull(grad_heads)
    grad_proj_low = grad_proj.astype(jnp.bfloat16)
    grad_wide_w = outer_dot(input_normalized, grad_proj_low)
    grad_in_part = inner_dot(grad_proj_low, back_wide)
    gain_first = jnp.sum(grad_in_part * scaled_in, axis=0)
    grad_in = grad_sum(grad_in_part)
    grad_tokens = grad_hidden + rms_back(tokens_in, grad_in * norm_first)
    query_cols = w_query.shape[1]
    value_cols = w_value.shape[1]
    grad_query = grad_wide_w[:, :query_cols]
    grad_key = grad_wide_w[:, query_cols : 2 * query_cols]
    grad_value = grad_wide_w[:, 2 * query_cols : 2 * query_cols + value_cols]
    grad_gate_out = grad_wide_w[:, 2 * query_cols + value_cols : 2 * query_cols + 2 * value_cols]
    grad_beta_decay = grad_wide_w[:, 2 * query_cols + 2 * value_cols :].reshape(
        model_width, 2, head_count
    )
    reduced = (
        lax.psum_scatter(
            grad_query.astype(jnp.bfloat16), "dp", scatter_dimension=0, tiled=True
        ).astype(jnp.float32),
        lax.psum_scatter(
            grad_key.astype(jnp.bfloat16), "dp", scatter_dimension=0, tiled=True
        ).astype(jnp.float32),
        lax.psum_scatter(
            grad_value.astype(jnp.bfloat16), "dp", scatter_dimension=0, tiled=True
        ).astype(jnp.float32),
        lax.psum_scatter(
            grad_gate_out.astype(jnp.bfloat16), "dp", scatter_dimension=0, tiled=True
        ).astype(jnp.float32),
        lax.psum_scatter(
            grad_beta_decay.astype(jnp.bfloat16), "dp", scatter_dimension=0, tiled=True
        ).astype(jnp.float32),
        lax.psum_scatter(
            grad_out_w.astype(jnp.bfloat16), "dp", scatter_dimension=1, tiled=True
        ).astype(jnp.float32),
        lax.psum_scatter(
            grad_pair_w[:, :ff_local].astype(jnp.bfloat16), "dp", scatter_dimension=0, tiled=True
        ).astype(jnp.float32),
        lax.psum_scatter(
            grad_pair_w[:, ff_local:].astype(jnp.bfloat16), "dp", scatter_dimension=0, tiled=True
        ).astype(jnp.float32),
        lax.psum_scatter(
            grad_down_w.astype(jnp.bfloat16), "dp", scatter_dimension=1, tiled=True
        ).astype(jnp.float32),
    )
    conv_full = lax.dynamic_update_slice_in_dim(
        jnp.zeros_like(conv_weight), grad_conv, head_start, 1
    )
    scale_full = lax.dynamic_update_slice_in_dim(jnp.zeros_like(a_log), grad_scale, head_start, 0)
    shift_full = lax.dynamic_update_slice_in_dim(jnp.zeros_like(dt_bias), grad_shift, head_start, 0)
    small_sums = lax.psum(
        (gain_first, conv_full, scale_full, shift_full, grad_gain, gain_mid), ("dp", "tensor")
    )
    return (
        layer_out,
        grad_tokens.reshape(tokens.shape),
        small_sums[0],
        reduced[0],
        reduced[1],
        reduced[2],
        reduced[3],
        reduced[4],
        small_sums[1],
        small_sums[2],
        small_sums[3],
        small_sums[4],
        reduced[5],
        small_sums[5],
        reduced[6],
        reduced[7],
        reduced[8],
    )


ALL = ("tensor", "dp")


def row_major(array):
    return with_layout_constraint(array, Layout(major_to_minor=tuple(range(array.ndim))))


def gather_all(shard):
    return row_major(lax.all_gather(row_major(shard), ALL, axis=0, tiled=False))


def scatter_all(parts):
    return row_major(lax.psum_scatter(row_major(parts), ALL, scatter_dimension=0, tiled=False))


def swap_core(array):
    return lax.ppermute(array, "tensor", [(i, i ^ 1) for i in range(lax.axis_size("tensor"))])


def swap_x(array):
    return lax.ppermute(array, "tensor", [(i, i ^ 2) for i in range(lax.axis_size("tensor"))])


def swap_y(array):
    return lax.ppermute(array, "dp", [(i, i ^ 1) for i in range(lax.axis_size("dp"))])


def swap_z(array, bit):
    return lax.ppermute(array, "dp", [(i, i ^ (2 * bit)) for i in range(lax.axis_size("dp"))])


def shift_z(array, offset):
    count = lax.axis_size("dp")
    return lax.ppermute(array, "dp", [(i, (i + 2 * offset) % count) for i in range(count)])


def sum_everywhere(array):
    array = array + swap_core(array)
    array = array + swap_x(array)
    array = array + swap_y(array)
    bit = 1
    while 2 * bit < lax.axis_size("dp"):
        array = array + swap_z(array, bit)
        bit *= 2
    return array


def in_rank_order(pair, other_pair):
    both = jnp.stack([pair, other_pair], axis=1).reshape((4,) + pair.shape[1:])
    rank = lax.axis_index("tensor")
    return jnp.stack(
        [lax.dynamic_index_in_dim(both, t ^ rank, 0, keepdims=False) for t in range(4)]
    )


def gather_tensor(own):
    pair = jnp.stack([own, swap_x(own)])
    return in_rank_order(pair, swap_core(pair))


def gather_steps(own):
    z_count = lax.axis_size("dp") // 2
    rank, place = lax.axis_index("tensor"), lax.axis_index("dp")
    z_own, y_own = place // 2, place % 2
    array = row_major(jnp.stack([own] + [shift_z(own, -r) for r in range(1, z_count)]))
    array = row_major(jnp.stack([array, swap_y(array)]))
    array = row_major(jnp.stack([array, swap_x(array)]))
    array = row_major(jnp.stack([array, swap_core(array)]))
    array = array.reshape((8 * z_count,) + own.shape)
    t = jnp.arange(4)[:, None] ^ rank
    i = jnp.arange(2 * z_count)[None, :]
    relative = (i // 2 - z_own) % z_count
    index = (((t % 2) * 2 + t // 2) * 2 + ((i % 2) ^ y_own)) * z_count + relative
    return row_major(jnp.take(array, index, axis=0, mode="clip"))


def low_sum(*members):
    total = members[0].astype(WIDE)
    for member in members[1:]:
        total = total + member.astype(WIDE)
    return row_major(total.astype(LOW))


def scatter_z(array):
    moved = [shift_z(row_major(array[r]), r) for r in range(1, array.shape[0])]
    total = array[0].astype(WIDE)
    for member in moved:
        total = total + member.astype(WIDE)
    return row_major(total)


def scatter_x_first(own, over_x, far_core):
    sent = swap_x(low_sum(over_x, far_core[1]))
    left = low_sum(own[1], far_core[0, 1], sent[1])
    sent_y = swap_y(left)
    return scatter_z(low_sum(own[0], far_core[0, 0], sent[0], sent_y))


def scatter_y_first(own, over_x, far_core):
    sent_x = swap_y(low_sum(over_x[1], far_core[1, 1]))
    sent_own = swap_y(low_sum(own[1], far_core[0, 1]))
    sent = swap_x(low_sum(over_x[0], far_core[1, 0], sent_x))
    return scatter_z(low_sum(own[0], far_core[0, 0], sent_own, sent))


def sequence_body(
    tokens,
    cotangent,
    live_count,
    norm_first,
    w_query,
    w_key,
    w_value,
    w_out_gate,
    w_beta_decay,
    conv_weight,
    a_log,
    dt_bias,
    out_gain,
    w_out,
    norm_second,
    w_gate,
    w_up,
    w_down,
):
    groups, owners = lax.axis_size("tensor"), lax.axis_size("dp")
    slot = lax.axis_index("tensor")
    slot_count, length, width = tokens.shape
    tap_count, all_heads, channels = conv_weight.shape
    value_dim = out_gain.shape[0]
    key_dim = (channels - value_dim) // 2
    heads = all_heads // groups
    sz = Sizes(length, heads, key_dim, value_dim)
    share = width // owners
    ff_local = w_gate.shape[1]

    wide_shard = jnp.concatenate([w_query, w_key, w_value, w_out_gate], axis=1)
    wide = gather_all(wide_shard).reshape(groups, owners, share, sz.cols)
    rates_rows = w_beta_decay.reshape(share, 2 * heads).T
    rates_rows = jnp.pad(rates_rows, ((0, -2 * heads % 16), (0, 0)))
    out_w = gather_steps(row_major(jnp.concatenate([w_out, rates_rows], axis=0)))
    small = out_w[:, :, heads * value_dim : heads * value_dim + 2 * heads]
    feed = gather_all(jnp.concatenate([w_gate.T, w_up.T, w_down], axis=0))
    feed = feed.reshape(groups, owners, 3, ff_local, share)

    tokens_in = lax.dynamic_index_in_dim(tokens, slot, 0, keepdims=False).astype(jnp.float32)
    cot_in = lax.dynamic_index_in_dim(cotangent, slot, 0, keepdims=False).astype(jnp.float32)
    grad_rows = cot_in * (slot < live_count[0]).astype(jnp.float32)
    grad_low = grad_rows.astype(LOW)
    scaled_in = unit_rms(tokens_in)
    normed_in = (scaled_in * norm_first).astype(LOW)

    small_cols = jnp.transpose(small, (1, 3, 0, 2)).reshape(width, groups * 2 * heads)
    rates = jnp.dot(normed_in, small_cols, preferred_element_type=jnp.float32)
    rates = rates.reshape(length, groups, 2, heads)
    scale = a_log.reshape(groups, heads)
    shift = dt_bias.reshape(groups, heads)

    def decays(rates, scale, shift):
        beta = jax.nn.sigmoid(rates[:, :, 0])
        gate_log = -jnp.exp(scale) * jax.nn.softplus(rates[:, :, 1] + shift)
        cum = jnp.cumsum(gate_log.reshape(-1, BLOCK, groups, heads), axis=1)
        tail = cum[:, -1:] - cum
        return (
            beta,
            cum.reshape(length, groups, heads),
            tail.reshape(length, groups, heads),
        )

    (beta, cum, tail), decays_pull = jax.vjp(decays, rates, scale, shift)
    col_form = jnp.moveaxis(jnp.concatenate([beta, cum, tail], axis=2), 1, 0)
    row_form = jnp.moveaxis(cum, 0, 2)
    taps = conv_weight.reshape(tap_count, groups, heads, channels)
    taps = jnp.moveaxis(taps, 1, 0)
    taps = jnp.concatenate(
        [
            taps[..., :key_dim].reshape(groups, tap_count, -1),
            taps[..., key_dim : 2 * key_dim].reshape(groups, tap_count, -1),
            taps[..., 2 * key_dim :].reshape(groups, tap_count, -1),
        ],
        axis=2,
    )
    gain_row = out_gain.reshape(1, value_dim)
    value_cols = heads * value_dim

    proj, mixed, o_rows, fresh, states, inverses = grouped_call(
        functools.partial(forward_kernel, sz),
        groups,
        [(normed_in, 0), (wide, 2), (taps, 2), (col_form, 2), (row_form, 2),
         (gain_row, 0)],
        [
            ((groups, length, sz.cols), jnp.float32, True),
            ((groups, length, value_cols), LOW, True),
            ((groups, length, value_cols), jnp.float32, True),
            ((groups, length, value_cols), LOW, True),
            ((groups, heads, sz.chunks, key_dim, value_dim), LOW, True),
            ((groups, heads, sz.stacks, sz.stack, sz.stack), LOW, True),
        ],
    )
    (branch_mix,) = grouped_call(
        out_kernel,
        groups,
        [(mixed, 2), (out_w, 2)],
        [((length, width), jnp.float32, False)],
    )
    hidden_res = tokens_in + branch_mix
    scaled_mid = unit_rms(hidden_res)
    normed_mid = (scaled_mid * norm_second).astype(LOW)
    branch_ff, grad_mid, grad_feed = grouped_call(
        feed_kernel,
        groups,
        [(normed_mid, 0), (grad_low, 0), (feed, 2)],
        [
            ((length, width), jnp.float32, False),
            ((length, width), jnp.float32, False),
            ((groups, owners, 3, ff_local, share), LOW, True),
        ],
    )
    feed_sum = scatter_all(grad_feed.reshape(groups * owners, 3 * ff_local, share))
    layer_own = (hidden_res + branch_ff).astype(LOW)

    gain_mid = jnp.sum(grad_mid * scaled_mid, axis=0)
    grad_hidden = grad_rows + rms_back(hidden_res, grad_mid * norm_second)
    grad_branch = grad_hidden.astype(LOW)
    z_count = owners // 2
    place = lax.axis_index("dp")
    near_first = jnp.array(
        [((place // 2 + z) % z_count) * 2 + (place % 2) ^ y for y in range(2) for z in range(z_count)]
    )

    def by_distance(rows):
        return jnp.take(rows.reshape(owners, share, -1), near_first, axis=0, mode="clip").reshape(width, -1)

    normed_far = by_distance(normed_in.T)
    branch_far = by_distance(grad_branch.T)

    def mix_back(core, first, count, flops, grad_branch):
        return grouped_call(
            functools.partial(backward_kernel, sz),
            count,
            [(normed_far, 0), (wide, 1), (out_w, 2), (grad_branch, 0), (branch_far, 0),
             (taps, 2), (col_form, 2), (row_form, 2), (gain_row, 0), (proj, 1), (mixed, 2),
             (o_rows, 2), (fresh, 2), (states, 2), (inverses, 2)],
            [
                ((count, owners, share, sz.conv_cols), LOW, True),
                ((count, owners, share, 2 * value_cols), LOW, True),
                ((length, width), jnp.float32, False),
                ((count, length, 128), jnp.float32, True),
                ((count, heads, length), jnp.float32, True),
                ((count, heads, sz.chunks, value_dim), jnp.float32, True),
                ((count, tap_count, sz.conv_cols), jnp.float32, True),
                ((1, value_dim), jnp.float32, False),
            ],
            scratch=[pltpu.VMEM((length, sz.cols), LOW)],
            flops=flops,
            rank=slot.astype(jnp.int32).reshape(1),
            group_of=lambda s, r: (2 * (s + first) + core) ^ r,
        )

    layer_x = swap_x(layer_own)
    far = mix_back(1, 0, 2, 1, grad_branch)
    grad_branch, layer_x, _ = lax.optimization_barrier((grad_branch, layer_x, far[7]))
    layer_pair = jnp.stack([layer_own, layer_x])
    layer_core = swap_core(layer_pair)
    far_conv, far_gate = swap_core(far[0]), swap_core(far[1])
    near_x = mix_back(0, 1, 1, 400_000_000_000, grad_branch)
    grad_branch, layer_core, far_conv, far_gate, _ = lax.optimization_barrier(
        (grad_branch, layer_core, far_conv, far_gate, near_x[7])
    )
    near_own = mix_back(0, 0, 1, 1, grad_branch)
    layer_out = in_rank_order(layer_pair, layer_core)
    by_owner = (-1, 2, z_count, share, 2 * value_cols)
    conv_owner = (-1, 2, z_count, share, sz.conv_cols)
    conv_sum = scatter_x_first(
        near_own[0].reshape(conv_owner)[0],
        near_x[0].reshape(conv_owner)[0],
        far_conv.reshape(conv_owner),
    )
    gate_sum = scatter_y_first(
        near_own[1].reshape(by_owner)[0],
        near_x[1].reshape(by_owner)[0],
        far_gate.reshape(by_owner),
    )
    grad_in = far[2] + near_x[2] + near_own[2]
    grad_gain = far[7] + near_x[7] + near_own[7]
    near = [jnp.concatenate([first, last]) for first, last in zip(near_own, near_x)]

    def in_order(near_part, far_part):
        both = jnp.stack([near_part, far_part], axis=1)
        both = both.reshape((groups,) + both.shape[2:])
        return jnp.take(both, jnp.arange(groups) ^ slot, axis=0, mode="clip")

    grad_cols, grad_row, grad_end, grad_taps = (
        in_order(near[k][..., : 3 * heads] if k == 3 else near[k],
                 far[k][..., : 3 * heads] if k == 3 else far[k])
        for k in (3, 4, 5, 6)
    )
    grad_cols = jnp.moveaxis(grad_cols, 0, 1)
    grad_beta = grad_cols[:, :, :heads]
    grad_tail = grad_cols[:, :, 2 * heads : 3 * heads]
    grad_cum = grad_cols[:, :, heads : 2 * heads] - jnp.moveaxis(grad_row, 2, 0)
    ends = jnp.moveaxis(jnp.sum(grad_end, axis=-1), 2, 0)
    last_of = (jnp.arange(length) % BLOCK == BLOCK - 1).astype(jnp.float32)
    ends = ends + jnp.sum(grad_tail.reshape(-1, BLOCK, groups, heads), axis=1)
    grad_cum = grad_cum + jnp.repeat(ends, BLOCK, axis=0) * last_of[:, None, None]
    grad_rates, grad_scale, grad_shift = decays_pull(
        (grad_beta, grad_cum, jnp.zeros_like(grad_cum))
    )
    rates_low = grad_rates.reshape(length, -1).astype(LOW)
    grad_small = outer_dot(normed_in, rates_low)
    grad_in = grad_in + inner_dot(rates_low, small_cols)
    gain_first = jnp.sum(grad_in * scaled_in, axis=0)
    grad_own = grad_hidden + rms_back(tokens_in, grad_in * norm_first)
    grad_tokens = gather_tensor(grad_own.astype(LOW))

    pieces = (gain_first, grad_taps, grad_scale, grad_shift, grad_gain, gain_mid, grad_small)
    flat = jnp.concatenate([member.reshape(-1) for member in pieces])
    flat = jnp.pad(flat, (0, -flat.shape[0] % 1024)).reshape(-1, 128)
    total = sum_everywhere(flat).reshape(-1)
    sums, start = [], 0
    for member in pieces:
        sums.append(total[start : start + member.size].reshape(member.shape))
        start += member.size
    gain_first, grad_taps, grad_scale, grad_shift, grad_gain, gain_mid, grad_small = sums
    key_cols = heads * key_dim
    grad_conv = jnp.concatenate(
        [
            grad_taps[:, :, :key_cols].reshape(groups, tap_count, heads, key_dim),
            grad_taps[:, :, key_cols : 2 * key_cols].reshape(groups, tap_count, heads, key_dim),
            grad_taps[:, :, 2 * key_cols :].reshape(groups, tap_count, heads, value_dim),
        ],
        axis=3,
    )
    grad_conv = jnp.moveaxis(grad_conv, 0, 1).reshape(conv_weight.shape)
    grad_small = lax.dynamic_slice(
        grad_small,
        (lax.axis_index("dp") * share, slot * 2 * heads),
        (share, 2 * heads),
    ).reshape(w_beta_decay.shape)
    feed_sum = feed_sum.astype(jnp.float32).reshape(3, ff_local, share)
    return (
        layer_out,
        grad_tokens.astype(jnp.float32),
        gain_first,
        conv_sum[:, :key_cols],
        conv_sum[:, key_cols : 2 * key_cols],
        conv_sum[:, 2 * key_cols :],
        gate_sum[:, :value_cols],
        grad_small,
        grad_conv,
        grad_scale.reshape(-1),
        grad_shift.reshape(-1),
        grad_gain.reshape(-1),
        gate_sum[:, value_cols:].T,
        gain_mid,
        feed_sum[0].T,
        feed_sum[1].T,
        feed_sum[2],
    )


def solution(mesh):
    in_specs = (
        P("dp", None, None),
        P("dp", None, None),
        P("dp"),
        P(),
        P("dp", "tensor"),
        P("dp", "tensor"),
        P("dp", "tensor"),
        P("dp", "tensor"),
        P("dp", None, "tensor"),
        P(),
        P(),
        P(),
        P(),
        P("tensor", "dp"),
        P(),
        P("dp", "tensor"),
        P("dp", "tensor"),
        P("tensor", "dp"),
    )
    out_specs = (
        P("dp", None, None),
        P("dp", None, None),
        P(),
        P("dp", "tensor"),
        P("dp", "tensor"),
        P("dp", "tensor"),
        P("dp", "tensor"),
        P("dp", None, "tensor"),
        P(),
        P(),
        P(),
        P(),
        P("tensor", "dp"),
        P(),
        P("dp", "tensor"),
        P("dp", "tensor"),
        P("tensor", "dp"),
    )
    def plan(*members):
        per_sequence = members[0].shape[0] == mesh.shape["tensor"] == 4
        return (sequence_body if per_sequence else body)(*members)

    return jax.shard_map(plan, mesh=mesh, in_specs=in_specs, out_specs=out_specs, check_vma=False)
```

```python
import functools

import jax
import jax.numpy as jnp
from jax import lax
from jax.experimental import pallas as pl
from jax.experimental.layout import Layout, with_layout_constraint
from jax.experimental.pallas import tpu as pltpu
from jax.sharding import PartitionSpec as P

BLOCK = 64


EPS = 1e-06


def exact_precision(form, first_op, second_op):
    return jnp.einsum(form, first_op, second_op, precision=lax.Precision.HIGHEST)


def unit_rms(values_in):
    return values_in * lax.rsqrt(jnp.mean(values_in * values_in, axis=-1, keepdims=True) + EPS)


def unit_length(values_in):
    return values_in * lax.rsqrt(jnp.sum(values_in * values_in, axis=-1, keepdims=True) + EPS)


def causal_conv(signal, tap_weights):
    result = signal * tap_weights[0]
    for offset in range(1, tap_weights.shape[0]):
        moved = jnp.pad(signal, ((0, 0), (offset, 0), (0, 0)))[:, : signal.shape[1], :]
        result = result + moved * tap_weights[offset]
    return result


def delta_rule(queries, key_rows, values, write_rate, gate_log):
    block_len = queries.shape[2]
    positions = jnp.arange(block_len)
    lower_mask = (positions[:, None] >= positions[None, :]).astype(jnp.float32)
    strict = (positions[:, None] > positions[None, :]).astype(jnp.float32)
    cumulate = jnp.cumsum(gate_log, axis=-1)
    spread = jnp.where(lower_mask > 0, cumulate[..., :, None] - cumulate[..., None, :], 0.0)
    decay_mat = jnp.exp(spread) * lower_mask
    key_beta = key_rows * write_rate[..., None]
    inner_prod = exact_precision("bnik,bnjk->bnij", key_beta, key_rows)
    nilpotent = -(inner_prod * decay_mat * strict)
    inverse = jnp.eye(block_len, dtype=jnp.float32) + nilpotent
    power_mat = nilpotent
    for doubling in range(block_len.bit_length() - 2):
        power_mat = exact_precision("bnij,bnjk->bnik", power_mat, power_mat)
        inverse = inverse + exact_precision("bnij,bnjk->bnik", inverse, power_mat)
    exp_cum = jnp.exp(cumulate)
    fresh_base = exact_precision("bnij,bnjv->bniv", inverse, values * write_rate[..., None])
    key_weight = exact_precision("bnij,bnjk->bnik", inverse, key_beta * exp_cum[..., None])
    scores = exact_precision("bnik,bnjk->bnij", queries, key_rows) * decay_mat
    query_decay = queries * exp_cum[..., None]
    ending = cumulate[..., -1]
    key_decay = key_rows * jnp.exp(ending[..., None] - cumulate)[..., None]

    def block_step(memory, pieces):
        base_n, weight_n, score_n, query_n, keyd_n, end_n = pieces
        fresh_val = base_n - exact_precision("bck,bkv->bcv", weight_n, memory)
        result = exact_precision("bck,bkv->bcv", query_n, memory) + exact_precision(
            "bcj,bjv->bcv", score_n, fresh_val
        )
        memory = memory * jnp.exp(end_n)[:, None, None] + exact_precision(
            "bck,bcv->bkv", keyd_n, fresh_val
        )
        return (memory, result)

    batch_size = queries.shape[0]
    memory_zero = jnp.zeros((batch_size, queries.shape[3], values.shape[3]), jnp.float32)
    pieces = tuple(
        (
            jnp.moveaxis(member, 1, 0)
            for member in (fresh_base, key_weight, scores, query_decay, key_decay, ending)
        )
    )
    _, results = lax.scan(jax.checkpoint(block_step), memory_zero, pieces)
    return jnp.moveaxis(results, 0, 1)


def mix_heads(projected_rows, conv_part, log_rate, rate_shift, gain_part):
    seq_count, length, _ = projected_rows.shape
    tap_count, head_count, channels = conv_part.shape
    value_dim = gain_part.shape[0]
    key_dim = (channels - value_dim) // 2
    key_cols = head_count * key_dim
    value_cols = head_count * value_dim
    query_in = projected_rows[..., :key_cols]
    key_in = projected_rows[..., key_cols : 2 * key_cols]
    value_in = projected_rows[..., 2 * key_cols : 2 * key_cols + value_cols]
    gate_in = projected_rows[..., 2 * key_cols + value_cols : 2 * key_cols + 2 * value_cols]
    write_in = projected_rows[
        ..., 2 * key_cols + 2 * value_cols : 2 * key_cols + 2 * value_cols + head_count
    ]
    decay_in = projected_rows[..., 2 * key_cols + 2 * value_cols + head_count :]
    queries = unit_length(
        jax.nn.silu(
            causal_conv(query_in, conv_part[:, :, :key_dim].reshape(tap_count, key_cols))
        ).reshape(seq_count, length, head_count, key_dim)
    ) * key_dim ** (-0.5)
    key_rows = unit_length(
        jax.nn.silu(
            causal_conv(key_in, conv_part[:, :, key_dim : 2 * key_dim].reshape(tap_count, key_cols))
        ).reshape(seq_count, length, head_count, key_dim)
    )
    values = jax.nn.silu(
        causal_conv(value_in, conv_part[:, :, 2 * key_dim :].reshape(tap_count, value_cols))
    ).reshape(seq_count, length, head_count, value_dim)
    write_rate = jax.nn.sigmoid(write_in)
    gate_log = -jnp.exp(log_rate) * jax.nn.softplus(decay_in + rate_shift)
    blocks = length // BLOCK

    def arrange(member):
        member = jnp.moveaxis(member, 2, 1)
        return member.reshape((seq_count * head_count, blocks, BLOCK) + member.shape[3:])

    result = delta_rule(
        arrange(queries), arrange(key_rows), arrange(values), arrange(write_rate), arrange(gate_log)
    )
    result = jnp.moveaxis(result.reshape(seq_count, head_count, length, value_dim), 1, 2)
    normed = (
        unit_rms(result)
        * gain_part
        * jax.nn.silu(gate_in.reshape(seq_count, length, head_count, value_dim))
    )
    return normed.reshape(seq_count, length, value_cols)


def outer_dot(first_op, second_op):
    return lax.dot_general(
        first_op, second_op, (((0,), (0,)), ((), ())), preferred_element_type=jnp.float32
    )


def inner_dot(first_op, second_op):
    return lax.dot_general(
        first_op, second_op, (((1,), (1,)), ((), ())), preferred_element_type=jnp.float32
    )


def rms_back(values_in, cotan):
    return jax.vjp(unit_rms, values_in)[1](cotan)[0]


def gather_first(shards):
    return (
        lax.all_gather(shards[0], "dp", axis=0, tiled=True),
        lax.all_gather(shards[1], "dp", axis=0, tiled=True),
        lax.all_gather(shards[2], "dp", axis=0, tiled=True),
        lax.all_gather(shards[3], "dp", axis=0, tiled=True),
        lax.all_gather(shards[4], "dp", axis=0, tiled=True),
        lax.all_gather(shards[5], "dp", axis=1, tiled=True),
        lax.all_gather(shards[6], "dp", axis=0, tiled=True),
        lax.all_gather(shards[7], "dp", axis=0, tiled=True),
        lax.all_gather(shards[8], "dp", axis=1, tiled=True),
    )


def gather_again(shards):
    return (
        lax.all_gather(shards[0], "dp", axis=0, tiled=True),
        lax.all_gather(shards[1], "dp", axis=0, tiled=True),
        lax.all_gather(shards[2], "dp", axis=0, tiled=True),
        lax.all_gather(shards[3], "dp", axis=0, tiled=True),
        lax.all_gather(shards[4], "dp", axis=0, tiled=True),
        lax.all_gather(shards[5], "dp", axis=1, tiled=True),
        lax.all_gather(shards[6], "dp", axis=0, tiled=True),
        lax.all_gather(shards[7], "dp", axis=0, tiled=True),
        lax.all_gather(shards[8], "dp", axis=1, tiled=True),
    )


def branch_sum(partial_rows):
    return lax.psum(partial_rows.astype(jnp.bfloat16), "tensor").astype(jnp.float32)


def grad_sum(partial_rows):
    return lax.psum(partial_rows.astype(jnp.bfloat16), "tensor").astype(jnp.float32)


def assemble(gathered, model_width):
    (
        full_query,
        full_key,
        full_value,
        full_gate_out,
        full_beta_decay,
        full_out,
        full_gate,
        full_up,
        full_down,
    ) = gathered
    widened_input = jnp.concatenate(
        [full_query, full_key, full_value, full_gate_out, full_beta_decay.reshape(model_width, -1)],
        axis=1,
    )
    paired_input = jnp.concatenate([full_gate, full_up], axis=1)
    return (widened_input, paired_input, full_out, full_down)


LOW = jnp.bfloat16
WIDE = jnp.float32
VMEM_BYTES = 58 * 1024 * 1024


def mxu(first_op, second_op, first_dim=1, second_dim=0):
    return lax.dot_general(
        first_op.astype(LOW),
        second_op.astype(LOW),
        (((first_dim,), (second_dim,)), ((), ())),
        preferred_element_type=WIDE,
    )


def mxu_split(first_op, second_op):
    first_high = first_op.astype(LOW)
    first_rest = (first_op - first_high.astype(WIDE)).astype(LOW)
    second_high = second_op.astype(LOW)
    second_rest = (second_op - second_high.astype(WIDE)).astype(LOW)
    return (
        mxu(first_high, second_high)
        + mxu(first_high, second_rest)
        + mxu(first_rest, second_high)
    )


def move_down(signal, offset):
    if offset == 0:
        return signal
    row = lax.broadcasted_iota(jnp.int32, signal.shape, 0)
    return jnp.where(row >= offset, pltpu.roll(signal, offset, 0), 0.0)


def move_up(signal, offset):
    if offset == 0:
        return signal
    length = signal.shape[0]
    row = lax.broadcasted_iota(jnp.int32, signal.shape, 0)
    return jnp.where(row < length - offset, pltpu.roll(signal, length - offset, 0), 0.0)


def conv_rows(signal, taps):
    result = signal * taps[0:1]
    for offset in range(1, taps.shape[0]):
        result = result + move_down(signal, offset) * taps[offset : offset + 1]
    return result


def conv_back(grad, signal, taps):
    result = grad * taps[0:1]
    for offset in range(1, taps.shape[0]):
        result = result + move_up(grad, offset) * taps[offset : offset + 1]
    tap_grads = [
        jnp.sum(grad * move_down(signal, offset), axis=0, keepdims=True)
        for offset in range(taps.shape[0])
    ]
    return result, tap_grads


def silu_back(values_in, sig):
    return sig * (1.0 + values_in * (1.0 - sig))


def block_masks(size):
    row = lax.broadcasted_iota(jnp.int32, (size, size), 0)
    col = lax.broadcasted_iota(jnp.int32, (size, size), 1)
    same = (row // BLOCK) == (col // BLOCK)
    return same & (row >= col), same & (row > col), row == col


def decay_of(lower, cum_col, cum_row):
    return jnp.where(lower, jnp.exp(jnp.where(lower, cum_col - cum_row, 0.0)), 0.0)


def unit_inverse(strict_part, eye):
    inverse = eye - strict_part
    power = -strict_part
    for _ in range(BLOCK.bit_length() - 2):
        power = mxu(power, power)
        inverse = inverse + mxu(inverse, power)
    rest = eye - inverse - mxu_split(strict_part, inverse)
    return inverse + mxu(inverse, rest)


class Sizes:
    def __init__(self, length, heads, key_dim, value_dim):
        self.length, self.heads, self.key_dim, self.value_dim = length, heads, key_dim, value_dim
        self.stack = min(256, length)
        self.stacks = length // self.stack
        self.chunks = length // BLOCK
        self.per_stack = self.stack // BLOCK
        self.conv_cols = heads * (2 * key_dim + value_dim)
        self.cols = self.conv_cols + heads * value_dim

    def parts(self, head):
        k, v, n = self.key_dim, self.value_dim, self.heads
        return (
            slice(head * k, (head + 1) * k),
            slice((n + head) * k, (n + head + 1) * k),
            slice(2 * n * k + head * v, 2 * n * k + (head + 1) * v),
            slice(2 * n * k + (n + head) * v, 2 * n * k + (n + head + 1) * v),
        )


def head_inputs(sz, proj_ref, taps_ref, head):
    q_at, k_at, v_at, _ = sz.parts(head)
    kept = []
    for at in (q_at, k_at, v_at):
        raw = proj_ref[0, :, at]
        taps = taps_ref[0, :, at]
        mixed = conv_rows(raw, taps)
        sig = jax.nn.sigmoid(mixed)
        kept.append((raw, taps, mixed, sig, mixed * sig))
    q_inv = lax.rsqrt(jnp.sum(kept[0][4] * kept[0][4], axis=-1, keepdims=True) + EPS)
    k_inv = lax.rsqrt(jnp.sum(kept[1][4] * kept[1][4], axis=-1, keepdims=True) + EPS)
    q_unit = kept[0][4] * q_inv
    keys = kept[1][4] * k_inv
    return kept, q_inv, k_inv, q_unit, keys, kept[2][4]


def forward_kernel(sz, x_ref, w_ref, taps_ref, col_ref, row_ref, gain_ref,
                   proj_ref, mixed_ref, o_ref, fresh_ref, state_ref, inv_ref):
    n = sz.heads
    depth = x_ref.shape[1]
    proj_ref[0] = mxu(x_ref[...], w_ref[0].reshape(depth, sz.cols))
    lower, strict, diag = block_masks(sz.stack)
    eye = diag.astype(WIDE)
    held = []
    for head in range(n):
        _, _, _, q_unit, keys, values = head_inputs(sz, proj_ref, taps_ref, head)
        queries = q_unit * (sz.key_dim ** -0.5)
        beta = col_ref[0, :, head : head + 1]
        cum = col_ref[0, :, n + head : n + head + 1]
        tail = col_ref[0, :, 2 * n + head : 2 * n + head + 1]
        q_low, k_low = queries.astype(LOW), keys.astype(LOW)
        scores, inverses = [], []
        for s in range(sz.stacks):
            at = slice(s * sz.stack, (s + 1) * sz.stack)
            decay = decay_of(lower, cum[at], row_ref[0, head : head + 1, at])
            inner = mxu(k_low[at], k_low[at], 1, 1) * decay * beta[at]
            inverse = unit_inverse(jnp.where(strict, inner, 0.0), eye)
            inv_ref[0, head, s] = inverse.astype(LOW)
            inverses.append(inverse.astype(LOW))
            scores.append((mxu(q_low[at], k_low[at], 1, 1) * decay).astype(LOW))
        exp_cum = jnp.exp(cum)
        key_tail = (keys * jnp.exp(tail)).astype(LOW)
        held.append((q_low, k_low, values, beta, cum, exp_cum, key_tail, scores, inverses))
    memory = [jnp.zeros((sz.key_dim, sz.value_dim), WIDE) for _ in range(n)]
    from_state = [[] for _ in range(n)]
    fresh = [[] for _ in range(n)]
    for c in range(sz.chunks):
        at = slice(c * BLOCK, (c + 1) * BLOCK)
        inner_at = slice((c % sz.per_stack) * BLOCK, (c % sz.per_stack + 1) * BLOCK)
        for head in range(n):
            q_low, k_low, values, beta, cum, exp_cum, key_tail, scores, inverses = held[head]
            memory_low = memory[head].astype(LOW)
            state_ref[0, head, c] = memory_low
            both = mxu(jnp.concatenate([k_low[at], q_low[at]], axis=0), memory_low)
            right = beta[at] * (values[at] - exp_cum[at] * both[:BLOCK])
            solved = mxu(inverses[c // sz.per_stack][inner_at, inner_at], right).astype(LOW)
            from_state[head].append(exp_cum[at] * both[BLOCK:])
            fresh[head].append(solved)
            last = slice((c + 1) * BLOCK - 1, (c + 1) * BLOCK)
            memory[head] = memory[head] * jnp.exp(cum[last]) + mxu(key_tail[at], solved, 0, 0)
    gain = gain_ref[...]
    for head in range(n):
        gate_at = sz.parts(head)[3]
        v_at = slice(head * sz.value_dim, (head + 1) * sz.value_dim)
        scores = held[head][7]
        for s in range(sz.stacks):
            at = slice(s * sz.stack, (s + 1) * sz.stack)
            of = slice(s * sz.per_stack, (s + 1) * sz.per_stack)
            solved = jnp.concatenate(fresh[head][of], axis=0)
            result = jnp.concatenate(from_state[head][of], axis=0) + mxu(scores[s], solved)
            fresh_ref[0, at, v_at] = solved
            o_ref[0, at, v_at] = result
            gate = proj_ref[0, at, gate_at]
            inv = lax.rsqrt(jnp.mean(result * result, axis=-1, keepdims=True) + EPS)
            mixed_ref[0, at, v_at] = (
                result * inv * gain * (gate * jax.nn.sigmoid(gate))
            ).astype(LOW)


def out_rows(wo_ref, count):
    return jnp.concatenate([wo_ref[0, i, :count] for i in range(wo_ref.shape[1])], axis=1)


def backward_kernel(sz, rank_ref, xt_ref, w_ref, wo_ref, gb_ref, gbt_ref, taps_ref, col_ref, row_ref,
                    gain_ref, proj_ref, mixed_ref, o_ref, fresh_ref, state_ref, inv_ref,
                    ga_ref, gb_out_ref, gin_ref, gcol_ref, grow_ref, gend_ref, gtaps_ref, ggain_ref,
                    gp_ref):
    n = sz.heads
    depth = xt_ref.shape[0]
    wo = out_rows(wo_ref, n * sz.value_dim)
    gate_cols = sz.cols - sz.conv_cols
    row_shape = ga_ref.shape[1:3]
    gb_out_ref[0, :, :, gate_cols:] = (
        mxu(gbt_ref[...], mixed_ref[0]).astype(LOW).reshape(row_shape + (gate_cols,))
    )
    grad_heads = mxu(gb_ref[...], wo, 1, 1)
    lower, strict, _ = block_masks(sz.stack)
    gain = gain_ref[...]
    step = pl.program_id(0)

    @pl.when(step == 0)
    def _():
        ggain_ref[...] = jnp.zeros_like(ggain_ref)
        gin_ref[...] = jnp.zeros_like(gin_ref)

    held = []
    for head in range(n):
        kept, q_inv, k_inv, q_unit, keys, values = head_inputs(sz, proj_ref, taps_ref, head)
        queries = q_unit * (sz.key_dim ** -0.5)
        v_at = slice(head * sz.value_dim, (head + 1) * sz.value_dim)
        gate_at = sz.parts(head)[3]
        gate = proj_ref[0, :, gate_at]
        sig = jax.nn.sigmoid(gate)
        result = o_ref[0, :, v_at]
        inv = lax.rsqrt(jnp.mean(result * result, axis=-1, keepdims=True) + EPS)
        unit = result * inv
        d_head = grad_heads[:, v_at]
        d_unit_gate = d_head * unit
        ggain_ref[...] += jnp.sum(d_unit_gate * (gate * sig), axis=0, keepdims=True)
        gp_ref[:, gate_at] = (d_unit_gate * gain * silu_back(gate, sig)).astype(LOW)
        d_unit = d_head * gain * (gate * sig)
        d_o = inv * (d_unit - unit * jnp.mean(d_unit * unit, axis=-1, keepdims=True))
        beta = col_ref[0, :, head : head + 1]
        cum = col_ref[0, :, n + head : n + head + 1]
        tail = col_ref[0, :, 2 * n + head : 2 * n + head + 1]
        q_low, k_low, do_low = queries.astype(LOW), keys.astype(LOW), d_o.astype(LOW)
        exp_cum, exp_tail = jnp.exp(cum), jnp.exp(tail)
        key_tail = keys * exp_tail
        decays, inners, scores, through = [], [], [], []
        for s in range(sz.stacks):
            at = slice(s * sz.stack, (s + 1) * sz.stack)
            decay = decay_of(lower, cum[at], row_ref[0, head : head + 1, at])
            score = mxu(q_low[at], k_low[at], 1, 1) * decay
            inners.append(jnp.where(strict, mxu(k_low[at], k_low[at], 1, 1) * decay, 0.0))
            decays.append(decay)
            scores.append(score)
            through.append(mxu(score, do_low[at], 0, 0))
        held.append(dict(
            kept=kept, q_inv=q_inv, k_inv=k_inv, q_unit=q_unit, keys=keys, values=values,
            d_o=d_o, do_low=do_low, beta=beta, cum=cum, q_low=q_low, k_low=k_low,
            exp_cum=exp_cum, exp_tail=exp_tail, key_tail=key_tail, decays=decays,
            inners=inners, scores=scores, through=through,
            d_right=[None] * sz.chunks, d_q=[None] * sz.chunks, d_k=[None] * sz.chunks,
            d_beta=[None] * sz.chunks, d_cum=[None] * sz.chunks, x=[None] * sz.chunks,
            d_v=[None] * sz.chunks,
        ))
    d_memory = [jnp.zeros((sz.key_dim, sz.value_dim), WIDE) for _ in range(n)]
    for c in reversed(range(sz.chunks)):
        at = slice(c * BLOCK, (c + 1) * BLOCK)
        s, local = c // sz.per_stack, c % sz.per_stack
        in_at = slice(local * BLOCK, (local + 1) * BLOCK)
        for head in range(n):
            m = held[head]
            v_at = slice(head * sz.value_dim, (head + 1) * sz.value_dim)
            memory_low = state_ref[0, head, c]
            grad_low = d_memory[head].astype(LOW)
            d_fresh = m["through"][s][in_at] + mxu(m["key_tail"][at], grad_low)
            d_right = mxu(inv_ref[0, head, s, in_at, in_at], d_fresh, 0, 0)
            d_z = m["beta"][at] * d_right
            lifted = m["exp_cum"][at] * m["d_o"][at]
            sunk = -m["exp_cum"][at] * d_z
            pair = jnp.concatenate([lifted.astype(LOW), sunk.astype(LOW)], axis=0)
            rows = jnp.concatenate([m["q_low"][at], m["k_low"][at]], axis=0)
            last = jnp.exp(m["cum"][(c + 1) * BLOCK - 1 : (c + 1) * BLOCK])
            gend_ref[0, head, c : c + 1, :] = last * jnp.sum(
                d_memory[head] * memory_low.astype(WIDE), axis=0, keepdims=True
            )
            d_tail = mxu(fresh_ref[0, at, v_at], grad_low, 1, 1)
            d_memory[head] = d_memory[head] * last + mxu(rows, pair, 0, 0)
            back = mxu(pair, memory_low, 1, 1)
            both = mxu(rows, memory_low)
            from_keys = m["exp_cum"][at] * both[BLOCK:]
            x = jnp.sum(d_tail * m["key_tail"][at], axis=-1, keepdims=True)
            m["x"][c] = x
            m["d_right"][c] = d_right
            m["d_v"][c] = d_z
            m["d_q"][c] = back[:BLOCK]
            m["d_k"][c] = back[BLOCK:] + d_tail * m["exp_tail"][at]
            m["d_beta"][c] = jnp.sum(
                d_right * (m["values"][at] - from_keys), axis=-1, keepdims=True
            )
            m["d_cum"][c] = (
                jnp.sum(lifted * both[:BLOCK], axis=-1, keepdims=True)
                - jnp.sum(d_z * from_keys, axis=-1, keepdims=True)
                - x
            )
    lane = lax.broadcasted_iota(jnp.int32, (sz.stack, gcol_ref.shape[2]), 1)
    columns = [jnp.zeros((sz.stack, gcol_ref.shape[2]), WIDE) for _ in range(sz.stacks)]
    for head in range(n):
        m = held[head]
        q_at, k_at, v_at, _ = sz.parts(head)
        own = slice(head * sz.value_dim, (head + 1) * sz.value_dim)
        d_q, d_k = [], []
        for s in range(sz.stacks):
            at = slice(s * sz.stack, (s + 1) * sz.stack)
            of = slice(s * sz.per_stack, (s + 1) * sz.per_stack)
            solved = fresh_ref[0, at, own]
            d_right = jnp.concatenate(m["d_right"][of], axis=0)
            d_score = mxu(m["do_low"][at], solved, 1, 1)
            d_inner = -jnp.where(strict, mxu(d_right, solved, 1, 1), 0.0)
            decay, inner, beta = m["decays"][s], m["inners"][s], m["beta"][at]
            d_qk = d_score * decay
            d_kk = d_inner * decay * beta
            by_beta = d_inner * inner
            spread = d_score * m["scores"][s] + by_beta * beta
            d_q.append(jnp.concatenate(m["d_q"][of], axis=0) + mxu(d_qk, m["k_low"][at]))
            d_k.append(
                jnp.concatenate(m["d_k"][of], axis=0)
                + mxu(d_qk, m["q_low"][at], 0, 0)
                + mxu(d_kk, m["k_low"][at], 0, 0)
                + mxu(d_kk, m["k_low"][at])
            )
            grow_ref[0, head : head + 1, at] = jnp.sum(spread, axis=0, keepdims=True)
            d_beta = jnp.concatenate(m["d_beta"][of], axis=0) + jnp.sum(
                by_beta, axis=-1, keepdims=True
            )
            d_cum = jnp.concatenate(m["d_cum"][of], axis=0) + jnp.sum(
                spread, axis=-1, keepdims=True
            )
            x = jnp.concatenate(m["x"][of], axis=0)
            columns[s] = jnp.where(lane == head, d_beta, columns[s])
            columns[s] = jnp.where(lane == n + head, d_cum, columns[s])
            columns[s] = jnp.where(lane == 2 * n + head, x, columns[s])
        d_q = jnp.concatenate(d_q, axis=0)
        d_k = jnp.concatenate(d_k, axis=0)
        d_v = jnp.concatenate(m["d_v"], axis=0)
        q_unit, keys = m["q_unit"], m["keys"]
        d_qs = (sz.key_dim ** -0.5) * m["q_inv"] * (
            d_q - q_unit * jnp.sum(d_q * q_unit, axis=-1, keepdims=True)
        )
        d_ks = m["k_inv"] * (d_k - keys * jnp.sum(d_k * keys, axis=-1, keepdims=True))
        for at, grad, (raw, taps, mixed, sig, _) in zip(
            (q_at, k_at, v_at), (d_qs, d_ks, d_v), m["kept"]
        ):
            d_raw, d_taps = conv_back(grad * silu_back(mixed, sig), raw, taps)
            gp_ref[:, at] = d_raw.astype(LOW)
            for j, member in enumerate(d_taps):
                gtaps_ref[0, j : j + 1, at] = member
    for s in range(sz.stacks):
        gcol_ref[0, s * sz.stack : (s + 1) * sz.stack] = columns[s]
    ga_ref[0] = mxu(xt_ref[...], gp_ref[:, : sz.conv_cols]).astype(LOW).reshape(ga_ref.shape[1:])
    gb_out_ref[0, :, :, :gate_cols] = (
        mxu(xt_ref[...], gp_ref[:, sz.conv_cols :]).astype(LOW).reshape(row_shape + (gate_cols,))
    )
    gin_ref[...] += mxu(gp_ref[...], w_ref[0].reshape(depth, sz.cols), 1, 1)


def out_kernel(mixed_ref, wo_ref, acc_ref):
    @pl.when(pl.program_id(0) == 0)
    def _():
        acc_ref[...] = jnp.zeros_like(acc_ref)

    acc_ref[...] += mxu(mixed_ref[0], out_rows(wo_ref, mixed_ref.shape[2]))


def feed_kernel(rank_ref, order_ref, n_ref, g_ref, w_ref, out_ref, gmid_ref, ga_ref, gb_ref, nf_ref, gf_ref):
    owners, _, width, share = w_ref.shape[1:]

    @pl.when(pl.program_id(0) == 0)
    def _():
        out_ref[...] = jnp.zeros_like(out_ref)
        gmid_ref[...] = jnp.zeros_like(gmid_ref)
        for p in range(owners):
            at = pl.ds(pl.multiple_of(order_ref[p] * share, share), share)
            nf_ref[:, p * share : (p + 1) * share] = n_ref[:, at]
            gf_ref[:, p * share : (p + 1) * share] = g_ref[:, at]

    def weight(which):
        return jnp.concatenate([w_ref[0, i, which] for i in range(owners)], axis=1)

    half = ga_ref.shape[2]
    cut = half - width

    def keep(ref, start, value):
        for p in range(owners):
            ref[0, p, start : start + value.shape[0]] = value[:, p * share : (p + 1) * share]

    rows, grads = n_ref[...], g_ref[...]
    w_gate, w_up, w_down = weight(0), weight(1), weight(2)
    gate = mxu(rows, w_gate, 1, 1)
    up = mxu(rows, w_up, 1, 1)
    sig = jax.nn.sigmoid(gate)
    act = (gate * sig * up).astype(LOW)
    out_ref[...] += mxu(act, w_down)
    d_act = mxu(grads, w_down, 1, 1)
    d_gate = (d_act * up * silu_back(gate, sig)).astype(LOW)
    d_up = (d_act * (gate * sig)).astype(LOW)
    gmid_ref[...] += mxu(d_gate, w_gate) + mxu(d_up, w_up)
    rows, grads = nf_ref[...], gf_ref[...]
    keep(ga_ref, 0, mxu(d_gate, rows, 0, 0).astype(LOW))
    grad_up = mxu(d_up, rows, 0, 0).astype(LOW)
    keep(ga_ref, width, grad_up[:cut])
    keep(gb_ref, 0, grad_up[cut:])
    keep(gb_ref, width - cut, mxu(act, grads, 0, 0).astype(LOW))


def grouped_call(kernel, steps, inputs, outputs, scratch=(), rank=None, group_of=None, flops=1):
    def spec(shape, by_group, buffers, place):
        rest = (0,) * (len(shape) - 1)
        if by_group:
            return pl.BlockSpec(
                (1,) + tuple(shape[1:]),
                lambda s, *r: (place(s, *r),) + rest,
                pipeline_mode=pl.Buffered(buffers),
            )
        return pl.BlockSpec(tuple(shape), lambda s, *r: (0,) + rest)

    def in_step(s, *r):
        return s

    in_place = in_step if group_of is None else lambda s, *r: group_of(s, r[0][0])
    prefetch = () if rank is None else rank
    return pl.pallas_call(
        kernel,
        grid_spec=pltpu.PrefetchScalarGridSpec(
            num_scalar_prefetch=len(prefetch),
            grid=(steps,),
            in_specs=[spec(a.shape, b > 0, b, in_place) for a, b in inputs],
            out_specs=[spec(s, by_group, 2, in_step) for s, _, by_group in outputs],
            scratch_shapes=list(scratch),
        ),
        out_shape=[jax.ShapeDtypeStruct(s, d) for s, d, _ in outputs],
        compiler_params=pltpu.CompilerParams(
            vmem_limit_bytes=VMEM_BYTES, dimension_semantics=("arbitrary",)
        ),
        cost_estimate=pl.CostEstimate(flops=flops, bytes_accessed=1, transcendentals=0),
    )(*prefetch, *[a for a, _ in inputs])


def body(
    tokens,
    cotangent,
    live_count,
    norm_first,
    w_query,
    w_key,
    w_value,
    w_out_gate,
    w_beta_decay,
    conv_weight,
    a_log,
    dt_bias,
    out_gain,
    w_out,
    norm_second,
    w_gate,
    w_up,
    w_down,
):
    slot_count, length, model_width = tokens.shape
    total_rows = slot_count * length
    head_count = a_log.shape[0] // lax.axis_size("tensor")
    head_start = lax.axis_index("tensor") * head_count
    conv_local = lax.dynamic_slice_in_dim(conv_weight, head_start, head_count, 1)
    decay_scale = lax.dynamic_slice_in_dim(a_log, head_start, head_count, 0)
    decay_shift = lax.dynamic_slice_in_dim(dt_bias, head_start, head_count, 0)
    shards = (w_query, w_key, w_value, w_out_gate, w_beta_decay, w_out, w_gate, w_up, w_down)
    widened_input, paired_input, out_proj, down_proj = assemble(gather_first(shards), model_width)
    tokens_in = tokens.reshape(total_rows, model_width).astype(jnp.float32)
    scaled_in = unit_rms(tokens_in)
    input_normalized = (scaled_in * norm_first).astype(jnp.bfloat16)
    projected_rows = jnp.dot(input_normalized, widened_input, preferred_element_type=jnp.float32)

    def mix_flat(proj_flat, conv_part, scale_part, shift_part, gain_part):
        return mix_heads(
            proj_flat.reshape(slot_count, length, -1), conv_part, scale_part, shift_part, gain_part
        ).reshape(total_rows, -1)

    mixed_heads, mix_pull = jax.vjp(
        mix_flat, projected_rows, conv_local, decay_scale, decay_shift, out_gain
    )
    mixed_low = mixed_heads.astype(jnp.bfloat16)
    hidden_res = tokens_in + branch_sum(
        jnp.dot(mixed_low, out_proj, preferred_element_type=jnp.float32)
    )
    scaled_mid = unit_rms(hidden_res)
    middle_normalized = (scaled_mid * norm_second).astype(jnp.bfloat16)
    gate_up_product = jnp.dot(middle_normalized, paired_input, preferred_element_type=jnp.float32)
    ff_local = paired_input.shape[1] // 2
    gate_part = gate_up_product[:, :ff_local]
    up_part = gate_up_product[:, ff_local:]
    sigmoid_gate = jax.nn.sigmoid(gate_part)
    silu_gate = gate_part * sigmoid_gate
    activated = (silu_gate * up_part).astype(jnp.bfloat16)
    result_rows = hidden_res + branch_sum(
        jnp.dot(activated, down_proj, preferred_element_type=jnp.float32)
    )
    layer_out = result_rows.astype(jnp.bfloat16).reshape(tokens.shape)
    live_rows = (jnp.arange(slot_count) < live_count[0]).astype(jnp.float32)
    grad_rows = (cotangent.astype(jnp.float32) * live_rows[:, None, None]).reshape(
        total_rows, model_width
    )
    back_wide, back_pair, back_out, back_down = assemble(gather_again(shards), model_width)
    grad_low = grad_rows.astype(jnp.bfloat16)
    grad_down_w = outer_dot(activated, grad_low)
    grad_act = inner_dot(grad_low, back_down)
    grad_gate = grad_act * up_part * sigmoid_gate * (1.0 + gate_part * (1.0 - sigmoid_gate))
    grad_up = grad_act * silu_gate
    grad_pair = jnp.concatenate([grad_gate, grad_up], axis=1).astype(jnp.bfloat16)
    grad_pair_w = outer_dot(middle_normalized, grad_pair)
    grad_mid_part = inner_dot(grad_pair, back_pair)
    gain_mid = jnp.sum(grad_mid_part * scaled_mid, axis=0)
    grad_mid = grad_sum(grad_mid_part)
    grad_hidden = grad_rows + rms_back(hidden_res, grad_mid * norm_second)
    grad_hidden_low = grad_hidden.astype(jnp.bfloat16)
    grad_out_w = outer_dot(mixed_low, grad_hidden_low)
    grad_heads = inner_dot(grad_hidden_low, back_out)
    grad_proj, grad_conv, grad_scale, grad_shift, grad_gain = mix_pull(grad_heads)
    grad_proj_low = grad_proj.astype(jnp.bfloat16)
    grad_wide_w = outer_dot(input_normalized, grad_proj_low)
    grad_in_part = inner_dot(grad_proj_low, back_wide)
    gain_first = jnp.sum(grad_in_part * scaled_in, axis=0)
    grad_in = grad_sum(grad_in_part)
    grad_tokens = grad_hidden + rms_back(tokens_in, grad_in * norm_first)
    query_cols = w_query.shape[1]
    value_cols = w_value.shape[1]
    grad_query = grad_wide_w[:, :query_cols]
    grad_key = grad_wide_w[:, query_cols : 2 * query_cols]
    grad_value = grad_wide_w[:, 2 * query_cols : 2 * query_cols + value_cols]
    grad_gate_out = grad_wide_w[:, 2 * query_cols + value_cols : 2 * query_cols + 2 * value_cols]
    grad_beta_decay = grad_wide_w[:, 2 * query_cols + 2 * value_cols :].reshape(
        model_width, 2, head_count
    )
    reduced = (
        lax.psum_scatter(
            grad_query.astype(jnp.bfloat16), "dp", scatter_dimension=0, tiled=True
        ).astype(jnp.float32),
        lax.psum_scatter(
            grad_key.astype(jnp.bfloat16), "dp", scatter_dimension=0, tiled=True
        ).astype(jnp.float32),
        lax.psum_scatter(
            grad_value.astype(jnp.bfloat16), "dp", scatter_dimension=0, tiled=True
        ).astype(jnp.float32),
        lax.psum_scatter(
            grad_gate_out.astype(jnp.bfloat16), "dp", scatter_dimension=0, tiled=True
        ).astype(jnp.float32),
        lax.psum_scatter(
            grad_beta_decay.astype(jnp.bfloat16), "dp", scatter_dimension=0, tiled=True
        ).astype(jnp.float32),
        lax.psum_scatter(
            grad_out_w.astype(jnp.bfloat16), "dp", scatter_dimension=1, tiled=True
        ).astype(jnp.float32),
        lax.psum_scatter(
            grad_pair_w[:, :ff_local].astype(jnp.bfloat16), "dp", scatter_dimension=0, tiled=True
        ).astype(jnp.float32),
        lax.psum_scatter(
            grad_pair_w[:, ff_local:].astype(jnp.bfloat16), "dp", scatter_dimension=0, tiled=True
        ).astype(jnp.float32),
        lax.psum_scatter(
            grad_down_w.astype(jnp.bfloat16), "dp", scatter_dimension=1, tiled=True
        ).astype(jnp.float32),
    )
    conv_full = lax.dynamic_update_slice_in_dim(
        jnp.zeros_like(conv_weight), grad_conv, head_start, 1
    )
    scale_full = lax.dynamic_update_slice_in_dim(jnp.zeros_like(a_log), grad_scale, head_start, 0)
    shift_full = lax.dynamic_update_slice_in_dim(jnp.zeros_like(dt_bias), grad_shift, head_start, 0)
    small_sums = lax.psum(
        (gain_first, conv_full, scale_full, shift_full, grad_gain, gain_mid), ("dp", "tensor")
    )
    return (
        layer_out,
        grad_tokens.reshape(tokens.shape),
        small_sums[0],
        reduced[0],
        reduced[1],
        reduced[2],
        reduced[3],
        reduced[4],
        small_sums[1],
        small_sums[2],
        small_sums[3],
        small_sums[4],
        reduced[5],
        small_sums[5],
        reduced[6],
        reduced[7],
        reduced[8],
    )


ALL = ("tensor", "dp")


def row_major(array):
    return with_layout_constraint(array, Layout(major_to_minor=tuple(range(array.ndim))))


def gather_all(shard):
    return row_major(lax.all_gather(row_major(shard), ALL, axis=0, tiled=False))


def swap_core(array):
    return lax.ppermute(array, "tensor", [(i, i ^ 1) for i in range(lax.axis_size("tensor"))])


def swap_x(array):
    return lax.ppermute(array, "tensor", [(i, i ^ 2) for i in range(lax.axis_size("tensor"))])


def swap_y(array):
    return lax.ppermute(array, "dp", [(i, i ^ 1) for i in range(lax.axis_size("dp"))])


def swap_z(array, bit):
    return lax.ppermute(array, "dp", [(i, i ^ (2 * bit)) for i in range(lax.axis_size("dp"))])


def shift_z(array, offset):
    count = lax.axis_size("dp")
    return lax.ppermute(array, "dp", [(i, (i + 2 * offset) % count) for i in range(count)])


def sum_everywhere(array):
    array = array + swap_core(array)
    array = array + swap_y(array)
    bit = 1
    while 2 * bit < lax.axis_size("dp"):
        array = array + swap_z(array, bit)
        bit *= 2
    return array + swap_x(array)


def in_rank_order(pair, other_pair):
    both = jnp.stack([pair, other_pair], axis=1).reshape((4,) + pair.shape[1:])
    rank = lax.axis_index("tensor")
    return jnp.stack(
        [lax.dynamic_index_in_dim(both, t ^ rank, 0, keepdims=False) for t in range(4)]
    )


def gather_steps(own):
    z_count = lax.axis_size("dp") // 2
    rank, place = lax.axis_index("tensor"), lax.axis_index("dp")
    z_own, y_own = place // 2, place % 2
    array = row_major(jnp.stack([own] + [shift_z(own, -r) for r in range(1, z_count)]))
    array = row_major(jnp.stack([array, swap_y(array)]))
    array = row_major(jnp.stack([array, swap_x(array)]))
    array = row_major(jnp.stack([array, swap_core(array)]))
    array = array.reshape((8 * z_count,) + own.shape)
    t = jnp.arange(4)[:, None] ^ rank
    i = jnp.arange(2 * z_count)[None, :]
    relative = (i // 2 - z_own) % z_count
    index = (((t % 2) * 2 + t // 2) * 2 + ((i % 2) ^ y_own)) * z_count + relative
    return row_major(jnp.take(array, index, axis=0, mode="clip"))


def low_sum(*members):
    total = members[0].astype(WIDE)
    for member in members[1:]:
        total = total + member.astype(WIDE)
    return row_major(total.astype(LOW))


def move_z(array):
    moved = [shift_z(row_major(array[r]), r) for r in range(1, array.shape[0])]
    return (row_major(array[0]),) + tuple(moved)


def sum_z(parts):
    total = parts[0].astype(WIDE)
    for member in parts[1:]:
        total = total + member.astype(WIDE)
    return row_major(total)


def after(array, *others):
    return lax.optimization_barrier((array, others))[0]


def sequence_body(
    tokens,
    cotangent,
    live_count,
    norm_first,
    w_query,
    w_key,
    w_value,
    w_out_gate,
    w_beta_decay,
    conv_weight,
    a_log,
    dt_bias,
    out_gain,
    w_out,
    norm_second,
    w_gate,
    w_up,
    w_down,
):
    groups, owners = lax.axis_size("tensor"), lax.axis_size("dp")
    slot = lax.axis_index("tensor")
    slot_count, length, width = tokens.shape
    tap_count, all_heads, channels = conv_weight.shape
    value_dim = out_gain.shape[0]
    key_dim = (channels - value_dim) // 2
    heads = all_heads // groups
    sz = Sizes(length, heads, key_dim, value_dim)
    share = width // owners
    ff_local = w_gate.shape[1]

    wide_shard = jnp.concatenate([w_query, w_key, w_value, w_out_gate], axis=1)
    wide = gather_all(wide_shard).reshape(groups, owners, share, sz.cols)
    rates_rows = w_beta_decay.reshape(share, 2 * heads).T
    rates_rows = jnp.pad(rates_rows, ((0, -2 * heads % 16), (0, 0)))
    out_w = gather_steps(row_major(jnp.concatenate([w_out, rates_rows], axis=0)))
    small = out_w[:, :, heads * value_dim : heads * value_dim + 2 * heads]
    feed = gather_all(jnp.concatenate([w_gate.T, w_up.T, w_down], axis=0))
    feed = feed.reshape(groups, owners, 3, ff_local, share)

    tokens_in = lax.dynamic_index_in_dim(tokens, slot, 0, keepdims=False).astype(jnp.float32)
    cot_in = lax.dynamic_index_in_dim(cotangent, slot, 0, keepdims=False).astype(jnp.float32)
    grad_rows = cot_in * (slot < live_count[0]).astype(jnp.float32)
    grad_low = grad_rows.astype(LOW)
    scaled_in = unit_rms(tokens_in)
    normed_in = (scaled_in * norm_first).astype(LOW)

    small_cols = jnp.transpose(small, (1, 3, 0, 2)).reshape(width, groups * 2 * heads)
    rates = jnp.dot(normed_in, small_cols, preferred_element_type=jnp.float32)
    rates = rates.reshape(length, groups, 2, heads)
    scale = a_log.reshape(groups, heads)
    shift = dt_bias.reshape(groups, heads)

    up_to = jnp.tril(jnp.ones((BLOCK, BLOCK), jnp.float32))

    def decays(rates, scale, shift):
        beta = jax.nn.sigmoid(rates[:, :, 0])
        gate_log = -jnp.exp(scale) * jax.nn.softplus(rates[:, :, 1] + shift)
        by_block = gate_log.reshape(-1, BLOCK, groups * heads)
        cum = exact_precision("ij,bjn->bin", up_to, by_block)
        tail = cum[:, -1:] - cum
        return (
            beta,
            cum.reshape(length, groups, heads),
            tail.reshape(length, groups, heads),
        )

    (beta, cum, tail), decays_pull = jax.vjp(decays, rates, scale, shift)
    col_form = jnp.moveaxis(jnp.concatenate([beta, cum, tail], axis=2), 1, 0)
    row_form = jnp.moveaxis(cum, 0, 2)
    taps = conv_weight.reshape(tap_count, groups, heads, channels)
    taps = jnp.moveaxis(taps, 1, 0)
    taps = jnp.concatenate(
        [
            taps[..., :key_dim].reshape(groups, tap_count, -1),
            taps[..., key_dim : 2 * key_dim].reshape(groups, tap_count, -1),
            taps[..., 2 * key_dim :].reshape(groups, tap_count, -1),
        ],
        axis=2,
    )
    gain_row = out_gain.reshape(1, value_dim)
    value_cols = heads * value_dim

    proj, mixed, o_rows, fresh, states, inverses = grouped_call(
        functools.partial(forward_kernel, sz),
        groups,
        [(normed_in, 0), (wide, 2), (taps, 2), (col_form, 2), (row_form, 2),
         (gain_row, 0)],
        [
            ((groups, length, sz.cols), jnp.float32, True),
            ((groups, length, value_cols), LOW, True),
            ((groups, length, value_cols), jnp.float32, True),
            ((groups, length, value_cols), LOW, True),
            ((groups, heads, sz.chunks, key_dim, value_dim), LOW, True),
            ((groups, heads, sz.stacks, sz.stack, sz.stack), LOW, True),
        ],
    )
    (branch_mix,) = grouped_call(
        out_kernel,
        groups,
        [(mixed, 2), (out_w, 2)],
        [((length, width), jnp.float32, False)],
    )
    hidden_res = tokens_in + branch_mix
    scaled_mid = unit_rms(hidden_res)
    normed_mid = (scaled_mid * norm_second).astype(LOW)
    z_count = owners // 2
    place = lax.axis_index("dp")
    near_first = jnp.array(
        [((place // 2 + z) % z_count) * 2 + (place % 2) ^ y for y in range(2) for z in range(z_count)]
    )

    rank = slot.astype(jnp.int32).reshape(1)
    half = 3 * ff_local // 2

    def feed_back(core, grads):
        return grouped_call(
            feed_kernel,
            groups // 2,
            [(normed_mid, 0), (grads, 0), (feed, 2)],
            [
                ((length, width), jnp.float32, False),
                ((length, width), jnp.float32, False),
                ((groups // 2, owners, half, share), LOW, True),
                ((groups // 2, owners, half, share), LOW, True),
            ],
            scratch=[pltpu.VMEM((length, width), LOW)] * 2,
            flops=400_000_000_000,
            rank=(rank, near_first.astype(jnp.int32)),
            group_of=lambda s, r: (2 * s + core) ^ r,
        )

    by_feed = (2, 2, z_count, half, share)
    feed_far = feed_back(1, grad_low)
    far_a, far_b = (swap_core(part).reshape(by_feed) for part in feed_far[2:])
    feed_near = feed_back(0, after(grad_low, feed_far[0]))
    near_a, near_b = (part.reshape(by_feed) for part in feed_near[2:])
    feed_x = swap_x(low_sum(near_a[1], far_a[1]))
    feed_y = swap_y(low_sum(near_b[:, 1], far_b[:, 1]))
    layer_own = (hidden_res + (feed_far[0] + feed_near[0])).astype(LOW)
    grad_mid = feed_far[1] + feed_near[1]

    gain_mid = jnp.sum(grad_mid * scaled_mid, axis=0)
    grad_hidden = grad_rows + rms_back(hidden_res, grad_mid * norm_second)
    grad_branch = grad_hidden.astype(LOW)
    def by_distance(rows):
        return jnp.take(rows.reshape(owners, share, -1), near_first, axis=0, mode="clip").reshape(width, -1)

    normed_far = by_distance(normed_in.T)
    branch_far = by_distance(grad_branch.T)

    def mix_back(core, first, count, flops, grad_branch):
        return grouped_call(
            functools.partial(backward_kernel, sz),
            count,
            [(normed_far, 0), (wide, 1), (out_w, 2), (grad_branch, 0), (branch_far, 0),
             (taps, 2), (col_form, 2), (row_form, 2), (gain_row, 0), (proj, 1), (mixed, 2),
             (o_rows, 2), (fresh, 2), (states, 2), (inverses, 2)],
            [
                ((count, owners, share, sz.conv_cols), LOW, True),
                ((count, owners, share, 2 * value_cols), LOW, True),
                ((length, width), jnp.float32, False),
                ((count, length, 128), jnp.float32, True),
                ((count, heads, length), jnp.float32, True),
                ((count, heads, sz.chunks, value_dim), jnp.float32, True),
                ((count, tap_count, sz.conv_cols), jnp.float32, True),
                ((1, value_dim), jnp.float32, False),
            ],
            scratch=[pltpu.VMEM((length, sz.cols), LOW)],
            flops=flops,
            rank=(rank,),
            group_of=lambda s, r: (2 * (s + first) + core) ^ r,
        )

    far = mix_back(1, 0, 2, 400_000_000_000, grad_branch)
    far_conv, far_gate = swap_core(far[0]), swap_core(far[1])
    grad_branch, feed_x, feed_y, _ = lax.optimization_barrier(
        (grad_branch, feed_x, feed_y, far[7])
    )
    feed_xy = swap_y(low_sum(near_a[0, 1], far_a[0, 1], feed_x[1]))
    feed_yx = swap_x(low_sum(near_b[1, 0], far_b[1, 0], feed_y[1]))
    near_x = mix_back(0, 1, 1, 400_000_000_000, grad_branch)
    grad_branch, feed_xy, feed_yx, far_conv, far_gate, _ = lax.optimization_barrier(
        (grad_branch, feed_xy, feed_yx, far_conv, far_gate, near_x[7])
    )
    by_gate = (-1, 2, z_count, share, 2 * value_cols)
    by_conv = (-1, 2, z_count, share, sz.conv_cols)
    far_conv, far_gate = far_conv.reshape(by_conv), far_gate.reshape(by_gate)
    over_conv, over_gate = near_x[0].reshape(by_conv)[0], near_x[1].reshape(by_gate)[0]
    to_conv_x = low_sum(over_conv, far_conv[1])
    to_gate_over = low_sum(over_gate[1], far_gate[1, 1])
    to_feed = jnp.concatenate(
        [
            low_sum(near_a[0, 0], far_a[0, 0], feed_x[0], feed_xy),
            low_sum(near_b[0, 0], far_b[0, 0], feed_y[0], feed_yx),
        ],
        axis=1,
    )
    grad_branch, to_conv_x, to_gate_over, to_feed = lax.optimization_barrier(
        (grad_branch, to_conv_x, to_gate_over, to_feed)
    )
    conv_x, gate_over = swap_x(to_conv_x), swap_y(to_gate_over)
    feed_parts = move_z(to_feed)
    near_own = mix_back(0, 0, 1, 400_000_000_000, grad_branch)
    own_conv, own_gate = near_own[0].reshape(by_conv)[0], near_own[1].reshape(by_gate)[0]
    rest, own_gate, gate_over = lax.optimization_barrier(
        (tuple(near_own[2:]), own_gate, gate_over)
    )
    gate_y = swap_y(low_sum(own_gate[1], far_gate[0, 1]))
    rest, conv_x, gate_y = lax.optimization_barrier((rest, conv_x, gate_y))
    to_conv_xy = low_sum(own_conv[1], far_conv[0, 1], conv_x[1])
    to_gate_yx = low_sum(over_gate[0], far_gate[1, 0], gate_over)
    rest, to_conv_xy, to_gate_yx = lax.optimization_barrier((rest, to_conv_xy, to_gate_yx))
    conv_xy, gate_yx = swap_y(to_conv_xy), swap_x(to_gate_yx)
    near_own = tuple(near_own[:2]) + rest
    grad_in = far[2] + near_x[2] + near_own[2]
    grad_gain = far[7] + near_x[7] + near_own[7]
    near = [jnp.concatenate([first, last]) for first, last in zip(near_own, near_x)]

    def in_order(near_part, far_part):
        both = jnp.stack([near_part, far_part], axis=1)
        both = both.reshape((groups,) + both.shape[2:])
        return jnp.take(both, jnp.arange(groups) ^ slot, axis=0, mode="clip")

    grad_cols, grad_row, grad_end, grad_taps = (
        in_order(near[k][..., : 3 * heads] if k == 3 else near[k],
                 far[k][..., : 3 * heads] if k == 3 else far[k])
        for k in (3, 4, 5, 6)
    )
    grad_cols = jnp.moveaxis(grad_cols, 0, 1)
    grad_beta = grad_cols[:, :, :heads]
    grad_tail = grad_cols[:, :, 2 * heads : 3 * heads]
    grad_cum = grad_cols[:, :, heads : 2 * heads] - jnp.moveaxis(grad_row, 2, 0)
    ends = jnp.moveaxis(jnp.sum(grad_end, axis=-1), 2, 0)
    last_of = (jnp.arange(length) % BLOCK == BLOCK - 1).astype(jnp.float32)
    ends = ends + jnp.sum(grad_tail.reshape(-1, BLOCK, groups, heads), axis=1)
    grad_cum = grad_cum + jnp.repeat(ends, BLOCK, axis=0) * last_of[:, None, None]
    grad_rates, grad_scale, grad_shift = decays_pull(
        (grad_beta, grad_cum, jnp.zeros_like(grad_cum))
    )
    rates_low = grad_rates.reshape(length, -1).astype(LOW)
    rates_low, conv_xy, gate_yx, feed_parts = lax.optimization_barrier(
        (rates_low, conv_xy, gate_yx, feed_parts)
    )
    feed_sum = sum_z(feed_parts)
    grad_small = outer_dot(normed_in, rates_low)
    grad_in = grad_in + inner_dot(rates_low, small_cols)
    gain_first = jnp.sum(grad_in * scaled_in, axis=0)
    grad_own = (grad_hidden + rms_back(tokens_in, grad_in * norm_first)).astype(LOW)

    pieces = (gain_first, grad_taps, grad_scale, grad_shift, grad_gain, gain_mid, grad_small)
    flat = jnp.concatenate([member.reshape(-1) for member in pieces])
    flat = jnp.pad(flat, (0, -flat.shape[0] % 1024)).reshape(-1, 128)
    to_mix = jnp.concatenate(
        [
            low_sum(own_conv[0], far_conv[0, 0], conv_x[0], conv_xy),
            low_sum(own_gate[0], far_gate[0, 0], gate_y, gate_yx),
        ],
        axis=1,
    )
    flat, to_mix, layer_own, grad_own = lax.optimization_barrier(
        (flat, to_mix, layer_own, grad_own)
    )
    mix_parts = move_z(to_mix)
    rows_own = jnp.stack([layer_own, grad_own])
    total = sum_everywhere(flat)
    rows_x, mix_parts, total = lax.optimization_barrier((swap_x(rows_own), mix_parts, total))
    rows_pair = jnp.stack([rows_own, rows_x])
    rows = in_rank_order(rows_pair, swap_core(rows_pair))
    layer_out, grad_tokens = rows[:, 0], rows[:, 1]
    mix_sum = sum_z(mix_parts)
    conv_sum, gate_sum = mix_sum[:share], mix_sum[share:]
    total = total.reshape(-1)
    sums, start = [], 0
    for member in pieces:
        sums.append(total[start : start + member.size].reshape(member.shape))
        start += member.size
    gain_first, grad_taps, grad_scale, grad_shift, grad_gain, gain_mid, grad_small = sums
    key_cols = heads * key_dim
    grad_conv = jnp.concatenate(
        [
            grad_taps[:, :, :key_cols].reshape(groups, tap_count, heads, key_dim),
            grad_taps[:, :, key_cols : 2 * key_cols].reshape(groups, tap_count, heads, key_dim),
            grad_taps[:, :, 2 * key_cols :].reshape(groups, tap_count, heads, value_dim),
        ],
        axis=3,
    )
    grad_conv = jnp.moveaxis(grad_conv, 0, 1).reshape(conv_weight.shape)
    grad_small = lax.dynamic_slice(
        grad_small,
        (lax.axis_index("dp") * share, slot * 2 * heads),
        (share, 2 * heads),
    ).reshape(w_beta_decay.shape)
    feed_sum = feed_sum.reshape(3, ff_local, share)
    return (
        layer_out,
        grad_tokens.astype(jnp.float32),
        gain_first,
        conv_sum[:, :key_cols],
        conv_sum[:, key_cols : 2 * key_cols],
        conv_sum[:, 2 * key_cols :],
        gate_sum[:, :value_cols],
        grad_small,
        grad_conv,
        grad_scale.reshape(-1),
        grad_shift.reshape(-1),
        grad_gain.reshape(-1),
        gate_sum[:, value_cols:].T,
        gain_mid,
        feed_sum[0].T,
        feed_sum[1].T,
        feed_sum[2],
    )


def solution(mesh):
    in_specs = (
        P("dp", None, None),
        P("dp", None, None),
        P("dp"),
        P(),
        P("dp", "tensor"),
        P("dp", "tensor"),
        P("dp", "tensor"),
        P("dp", "tensor"),
        P("dp", None, "tensor"),
        P(),
        P(),
        P(),
        P(),
        P("tensor", "dp"),
        P(),
        P("dp", "tensor"),
        P("dp", "tensor"),
        P("tensor", "dp"),
    )
    out_specs = (
        P("dp", None, None),
        P("dp", None, None),
        P(),
        P("dp", "tensor"),
        P("dp", "tensor"),
        P("dp", "tensor"),
        P("dp", "tensor"),
        P("dp", None, "tensor"),
        P(),
        P(),
        P(),
        P(),
        P("tensor", "dp"),
        P(),
        P("dp", "tensor"),
        P("dp", "tensor"),
        P("tensor", "dp"),
    )
    def plan(*members):
        per_sequence = members[0].shape[0] == mesh.shape["tensor"] == 4
        return (sequence_body if per_sequence else body)(*members)

    return jax.shard_map(plan, mesh=mesh, in_specs=in_specs, out_specs=out_specs, check_vma=False)
```

```python
import functools

import jax
import jax.numpy as jnp
from jax import lax
from jax.experimental import pallas as pl
from jax.experimental.layout import Layout, with_layout_constraint
from jax.experimental.pallas import tpu as pltpu
from jax.sharding import PartitionSpec as P

BLOCK = 64


EPS = 1e-06


def exact_precision(form, first_op, second_op):
    return jnp.einsum(form, first_op, second_op, precision=lax.Precision.HIGHEST)


def unit_rms(values_in):
    return values_in * lax.rsqrt(jnp.mean(values_in * values_in, axis=-1, keepdims=True) + EPS)


def unit_length(values_in):
    return values_in * lax.rsqrt(jnp.sum(values_in * values_in, axis=-1, keepdims=True) + EPS)


def causal_conv(signal, tap_weights):
    result = signal * tap_weights[0]
    for offset in range(1, tap_weights.shape[0]):
        moved = jnp.pad(signal, ((0, 0), (offset, 0), (0, 0)))[:, : signal.shape[1], :]
        result = result + moved * tap_weights[offset]
    return result


def delta_rule(queries, key_rows, values, write_rate, gate_log):
    block_len = queries.shape[2]
    positions = jnp.arange(block_len)
    lower_mask = (positions[:, None] >= positions[None, :]).astype(jnp.float32)
    strict = (positions[:, None] > positions[None, :]).astype(jnp.float32)
    cumulate = jnp.cumsum(gate_log, axis=-1)
    spread = jnp.where(lower_mask > 0, cumulate[..., :, None] - cumulate[..., None, :], 0.0)
    decay_mat = jnp.exp(spread) * lower_mask
    key_beta = key_rows * write_rate[..., None]
    inner_prod = exact_precision("bnik,bnjk->bnij", key_beta, key_rows)
    nilpotent = -(inner_prod * decay_mat * strict)
    inverse = jnp.eye(block_len, dtype=jnp.float32) + nilpotent
    power_mat = nilpotent
    for doubling in range(block_len.bit_length() - 2):
        power_mat = exact_precision("bnij,bnjk->bnik", power_mat, power_mat)
        inverse = inverse + exact_precision("bnij,bnjk->bnik", inverse, power_mat)
    exp_cum = jnp.exp(cumulate)
    fresh_base = exact_precision("bnij,bnjv->bniv", inverse, values * write_rate[..., None])
    key_weight = exact_precision("bnij,bnjk->bnik", inverse, key_beta * exp_cum[..., None])
    scores = exact_precision("bnik,bnjk->bnij", queries, key_rows) * decay_mat
    query_decay = queries * exp_cum[..., None]
    ending = cumulate[..., -1]
    key_decay = key_rows * jnp.exp(ending[..., None] - cumulate)[..., None]

    def block_step(memory, pieces):
        base_n, weight_n, score_n, query_n, keyd_n, end_n = pieces
        fresh_val = base_n - exact_precision("bck,bkv->bcv", weight_n, memory)
        result = exact_precision("bck,bkv->bcv", query_n, memory) + exact_precision(
            "bcj,bjv->bcv", score_n, fresh_val
        )
        memory = memory * jnp.exp(end_n)[:, None, None] + exact_precision(
            "bck,bcv->bkv", keyd_n, fresh_val
        )
        return (memory, result)

    batch_size = queries.shape[0]
    memory_zero = jnp.zeros((batch_size, queries.shape[3], values.shape[3]), jnp.float32)
    pieces = tuple(
        (
            jnp.moveaxis(member, 1, 0)
            for member in (fresh_base, key_weight, scores, query_decay, key_decay, ending)
        )
    )
    _, results = lax.scan(jax.checkpoint(block_step), memory_zero, pieces)
    return jnp.moveaxis(results, 0, 1)


def mix_heads(projected_rows, conv_part, log_rate, rate_shift, gain_part):
    seq_count, length, _ = projected_rows.shape
    tap_count, head_count, channels = conv_part.shape
    value_dim = gain_part.shape[0]
    key_dim = (channels - value_dim) // 2
    key_cols = head_count * key_dim
    value_cols = head_count * value_dim
    query_in = projected_rows[..., :key_cols]
    key_in = projected_rows[..., key_cols : 2 * key_cols]
    value_in = projected_rows[..., 2 * key_cols : 2 * key_cols + value_cols]
    gate_in = projected_rows[..., 2 * key_cols + value_cols : 2 * key_cols + 2 * value_cols]
    write_in = projected_rows[
        ..., 2 * key_cols + 2 * value_cols : 2 * key_cols + 2 * value_cols + head_count
    ]
    decay_in = projected_rows[..., 2 * key_cols + 2 * value_cols + head_count :]
    queries = unit_length(
        jax.nn.silu(
            causal_conv(query_in, conv_part[:, :, :key_dim].reshape(tap_count, key_cols))
        ).reshape(seq_count, length, head_count, key_dim)
    ) * key_dim ** (-0.5)
    key_rows = unit_length(
        jax.nn.silu(
            causal_conv(key_in, conv_part[:, :, key_dim : 2 * key_dim].reshape(tap_count, key_cols))
        ).reshape(seq_count, length, head_count, key_dim)
    )
    values = jax.nn.silu(
        causal_conv(value_in, conv_part[:, :, 2 * key_dim :].reshape(tap_count, value_cols))
    ).reshape(seq_count, length, head_count, value_dim)
    write_rate = jax.nn.sigmoid(write_in)
    gate_log = -jnp.exp(log_rate) * jax.nn.softplus(decay_in + rate_shift)
    blocks = length // BLOCK

    def arrange(member):
        member = jnp.moveaxis(member, 2, 1)
        return member.reshape((seq_count * head_count, blocks, BLOCK) + member.shape[3:])

    result = delta_rule(
        arrange(queries), arrange(key_rows), arrange(values), arrange(write_rate), arrange(gate_log)
    )
    result = jnp.moveaxis(result.reshape(seq_count, head_count, length, value_dim), 1, 2)
    normed = (
        unit_rms(result)
        * gain_part
        * jax.nn.silu(gate_in.reshape(seq_count, length, head_count, value_dim))
    )
    return normed.reshape(seq_count, length, value_cols)


def outer_dot(first_op, second_op):
    return lax.dot_general(
        first_op, second_op, (((0,), (0,)), ((), ())), preferred_element_type=jnp.float32
    )


def inner_dot(first_op, second_op):
    return lax.dot_general(
        first_op, second_op, (((1,), (1,)), ((), ())), preferred_element_type=jnp.float32
    )


def rms_back(values_in, cotan):
    return jax.vjp(unit_rms, values_in)[1](cotan)[0]


def gather_first(shards):
    return (
        lax.all_gather(shards[0], "dp", axis=0, tiled=True),
        lax.all_gather(shards[1], "dp", axis=0, tiled=True),
        lax.all_gather(shards[2], "dp", axis=0, tiled=True),
        lax.all_gather(shards[3], "dp", axis=0, tiled=True),
        lax.all_gather(shards[4], "dp", axis=0, tiled=True),
        lax.all_gather(shards[5], "dp", axis=1, tiled=True),
        lax.all_gather(shards[6], "dp", axis=0, tiled=True),
        lax.all_gather(shards[7], "dp", axis=0, tiled=True),
        lax.all_gather(shards[8], "dp", axis=1, tiled=True),
    )


def gather_again(shards):
    return (
        lax.all_gather(shards[0], "dp", axis=0, tiled=True),
        lax.all_gather(shards[1], "dp", axis=0, tiled=True),
        lax.all_gather(shards[2], "dp", axis=0, tiled=True),
        lax.all_gather(shards[3], "dp", axis=0, tiled=True),
        lax.all_gather(shards[4], "dp", axis=0, tiled=True),
        lax.all_gather(shards[5], "dp", axis=1, tiled=True),
        lax.all_gather(shards[6], "dp", axis=0, tiled=True),
        lax.all_gather(shards[7], "dp", axis=0, tiled=True),
        lax.all_gather(shards[8], "dp", axis=1, tiled=True),
    )


def branch_sum(partial_rows):
    return lax.psum(partial_rows.astype(jnp.bfloat16), "tensor").astype(jnp.float32)


def grad_sum(partial_rows):
    return lax.psum(partial_rows.astype(jnp.bfloat16), "tensor").astype(jnp.float32)


def assemble(gathered, model_width):
    (
        full_query,
        full_key,
        full_value,
        full_gate_out,
        full_beta_decay,
        full_out,
        full_gate,
        full_up,
        full_down,
    ) = gathered
    widened_input = jnp.concatenate(
        [full_query, full_key, full_value, full_gate_out, full_beta_decay.reshape(model_width, -1)],
        axis=1,
    )
    paired_input = jnp.concatenate([full_gate, full_up], axis=1)
    return (widened_input, paired_input, full_out, full_down)


LOW = jnp.bfloat16
WIDE = jnp.float32
VMEM_BYTES = 58 * 1024 * 1024


def mxu(first_op, second_op, first_dim=1, second_dim=0):
    return lax.dot_general(
        first_op.astype(LOW),
        second_op.astype(LOW),
        (((first_dim,), (second_dim,)), ((), ())),
        preferred_element_type=WIDE,
    )


def mxu_split(first_op, second_op):
    first_high = first_op.astype(LOW)
    first_rest = (first_op - first_high.astype(WIDE)).astype(LOW)
    second_high = second_op.astype(LOW)
    second_rest = (second_op - second_high.astype(WIDE)).astype(LOW)
    return (
        mxu(first_high, second_high)
        + mxu(first_high, second_rest)
        + mxu(first_rest, second_high)
    )


def move_down(signal, offset):
    if offset == 0:
        return signal
    row = lax.broadcasted_iota(jnp.int32, signal.shape, 0)
    return jnp.where(row >= offset, pltpu.roll(signal, offset, 0), 0.0)


def move_up(signal, offset):
    if offset == 0:
        return signal
    length = signal.shape[0]
    row = lax.broadcasted_iota(jnp.int32, signal.shape, 0)
    return jnp.where(row < length - offset, pltpu.roll(signal, length - offset, 0), 0.0)


def conv_rows(signal, taps):
    result = signal * taps[0:1]
    for offset in range(1, taps.shape[0]):
        result = result + move_down(signal, offset) * taps[offset : offset + 1]
    return result


def conv_back(grad, signal, taps):
    result = grad * taps[0:1]
    for offset in range(1, taps.shape[0]):
        result = result + move_up(grad, offset) * taps[offset : offset + 1]
    tap_grads = [
        jnp.sum(grad * move_down(signal, offset), axis=0, keepdims=True)
        for offset in range(taps.shape[0])
    ]
    return result, tap_grads


def silu_back(values_in, sig):
    return sig * (1.0 + values_in * (1.0 - sig))


def block_masks(size):
    row = lax.broadcasted_iota(jnp.int32, (size, size), 0)
    col = lax.broadcasted_iota(jnp.int32, (size, size), 1)
    same = (row // BLOCK) == (col // BLOCK)
    return same & (row >= col), same & (row > col), row == col


def decay_of(lower, cum_col, cum_row):
    return jnp.where(lower, jnp.exp(jnp.where(lower, cum_col - cum_row, 0.0)), 0.0)


def unit_inverse(strict_part, eye):
    inverse = eye - strict_part
    power = -strict_part
    for _ in range(BLOCK.bit_length() - 2):
        power = mxu(power, power)
        inverse = inverse + mxu(inverse, power)
    rest = eye - inverse - mxu_split(strict_part, inverse)
    return inverse + mxu(inverse, rest)


class Sizes:
    def __init__(self, length, heads, key_dim, value_dim):
        self.length, self.heads, self.key_dim, self.value_dim = length, heads, key_dim, value_dim
        self.stack = min(256, length)
        self.stacks = length // self.stack
        self.chunks = length // BLOCK
        self.per_stack = self.stack // BLOCK
        self.conv_cols = heads * (2 * key_dim + value_dim)
        self.cols = self.conv_cols + heads * value_dim

    def parts(self, head):
        k, v, n = self.key_dim, self.value_dim, self.heads
        return (
            slice(head * k, (head + 1) * k),
            slice((n + head) * k, (n + head + 1) * k),
            slice(2 * n * k + head * v, 2 * n * k + (head + 1) * v),
            slice(2 * n * k + (n + head) * v, 2 * n * k + (n + head + 1) * v),
        )


def head_inputs(sz, proj_ref, taps_ref, head):
    q_at, k_at, v_at, _ = sz.parts(head)
    kept = []
    for at in (q_at, k_at, v_at):
        raw = proj_ref[0, :, at]
        taps = taps_ref[0, :, at]
        mixed = conv_rows(raw, taps)
        sig = jax.nn.sigmoid(mixed)
        kept.append((raw, taps, mixed, sig, mixed * sig))
    q_inv = lax.rsqrt(jnp.sum(kept[0][4] * kept[0][4], axis=-1, keepdims=True) + EPS)
    k_inv = lax.rsqrt(jnp.sum(kept[1][4] * kept[1][4], axis=-1, keepdims=True) + EPS)
    q_unit = kept[0][4] * q_inv
    keys = kept[1][4] * k_inv
    return kept, q_inv, k_inv, q_unit, keys, kept[2][4]


def forward_kernel(sz, x_ref, w_ref, taps_ref, col_ref, row_ref, gain_ref,
                   proj_ref, mixed_ref, o_ref, fresh_ref, state_ref, inv_ref):
    n = sz.heads
    depth = x_ref.shape[1]
    proj_ref[0] = mxu(x_ref[...], w_ref[0].reshape(depth, sz.cols))
    lower, strict, diag = block_masks(sz.stack)
    eye = diag.astype(WIDE)
    held = []
    for head in range(n):
        _, _, _, q_unit, keys, values = head_inputs(sz, proj_ref, taps_ref, head)
        queries = q_unit * (sz.key_dim ** -0.5)
        beta = col_ref[0, :, head : head + 1]
        cum = col_ref[0, :, n + head : n + head + 1]
        tail = col_ref[0, :, 2 * n + head : 2 * n + head + 1]
        q_low, k_low = queries.astype(LOW), keys.astype(LOW)
        scores, inverses = [], []
        for s in range(sz.stacks):
            at = slice(s * sz.stack, (s + 1) * sz.stack)
            decay = decay_of(lower, cum[at], row_ref[0, head : head + 1, at])
            inner = mxu(k_low[at], k_low[at], 1, 1) * decay * beta[at]
            inverse = unit_inverse(jnp.where(strict, inner, 0.0), eye)
            inv_ref[0, head, s] = inverse.astype(LOW)
            inverses.append(inverse.astype(LOW))
            scores.append((mxu(q_low[at], k_low[at], 1, 1) * decay).astype(LOW))
        exp_cum = jnp.exp(cum)
        key_tail = (keys * jnp.exp(tail)).astype(LOW)
        held.append((q_low, k_low, values, beta, cum, exp_cum, key_tail, scores, inverses))
    memory = [jnp.zeros((sz.key_dim, sz.value_dim), WIDE) for _ in range(n)]
    from_state = [[] for _ in range(n)]
    fresh = [[] for _ in range(n)]
    for c in range(sz.chunks):
        at = slice(c * BLOCK, (c + 1) * BLOCK)
        inner_at = slice((c % sz.per_stack) * BLOCK, (c % sz.per_stack + 1) * BLOCK)
        for head in range(n):
            q_low, k_low, values, beta, cum, exp_cum, key_tail, scores, inverses = held[head]
            memory_low = memory[head].astype(LOW)
            state_ref[0, head, c] = memory_low
            both = mxu(jnp.concatenate([k_low[at], q_low[at]], axis=0), memory_low)
            right = beta[at] * (values[at] - exp_cum[at] * both[:BLOCK])
            solved = mxu(inverses[c // sz.per_stack][inner_at, inner_at], right).astype(LOW)
            from_state[head].append(exp_cum[at] * both[BLOCK:])
            fresh[head].append(solved)
            last = slice((c + 1) * BLOCK - 1, (c + 1) * BLOCK)
            memory[head] = memory[head] * jnp.exp(cum[last]) + mxu(key_tail[at], solved, 0, 0)
    gain = gain_ref[...]
    for head in range(n):
        gate_at = sz.parts(head)[3]
        v_at = slice(head * sz.value_dim, (head + 1) * sz.value_dim)
        scores = held[head][7]
        for s in range(sz.stacks):
            at = slice(s * sz.stack, (s + 1) * sz.stack)
            of = slice(s * sz.per_stack, (s + 1) * sz.per_stack)
            solved = jnp.concatenate(fresh[head][of], axis=0)
            result = jnp.concatenate(from_state[head][of], axis=0) + mxu(scores[s], solved)
            fresh_ref[0, at, v_at] = solved
            o_ref[0, at, v_at] = result
            gate = proj_ref[0, at, gate_at]
            inv = lax.rsqrt(jnp.mean(result * result, axis=-1, keepdims=True) + EPS)
            mixed_ref[0, at, v_at] = (
                result * inv * gain * (gate * jax.nn.sigmoid(gate))
            ).astype(LOW)


def out_rows(wo_ref, count):
    return jnp.concatenate([wo_ref[0, i, :count] for i in range(wo_ref.shape[1])], axis=1)


def backward_kernel(sz, rank_ref, xt_ref, w_ref, wo_ref, gb_ref, gbt_ref, taps_ref, col_ref, row_ref,
                    gain_ref, proj_ref, mixed_ref, o_ref, fresh_ref, state_ref, inv_ref,
                    ga_ref, gb_out_ref, gin_ref, gcol_ref, grow_ref, gend_ref, gtaps_ref, ggain_ref,
                    gp_ref):
    n = sz.heads
    depth = xt_ref.shape[0]
    wo = out_rows(wo_ref, n * sz.value_dim)
    gate_cols = sz.cols - sz.conv_cols
    row_shape = ga_ref.shape[1:3]
    gb_out_ref[0, :, :, gate_cols:] = (
        mxu(gbt_ref[...], mixed_ref[0]).astype(LOW).reshape(row_shape + (gate_cols,))
    )
    grad_heads = mxu(gb_ref[...], wo, 1, 1)
    lower, strict, _ = block_masks(sz.stack)
    gain = gain_ref[...]
    step = pl.program_id(0)

    @pl.when(step == 0)
    def _():
        ggain_ref[...] = jnp.zeros_like(ggain_ref)
        gin_ref[...] = jnp.zeros_like(gin_ref)

    held = []
    for head in range(n):
        kept, q_inv, k_inv, q_unit, keys, values = head_inputs(sz, proj_ref, taps_ref, head)
        queries = q_unit * (sz.key_dim ** -0.5)
        v_at = slice(head * sz.value_dim, (head + 1) * sz.value_dim)
        gate_at = sz.parts(head)[3]
        gate = proj_ref[0, :, gate_at]
        sig = jax.nn.sigmoid(gate)
        result = o_ref[0, :, v_at]
        inv = lax.rsqrt(jnp.mean(result * result, axis=-1, keepdims=True) + EPS)
        unit = result * inv
        d_head = grad_heads[:, v_at]
        d_unit_gate = d_head * unit
        ggain_ref[...] += jnp.sum(d_unit_gate * (gate * sig), axis=0, keepdims=True)
        gp_ref[:, gate_at] = (d_unit_gate * gain * silu_back(gate, sig)).astype(LOW)
        d_unit = d_head * gain * (gate * sig)
        d_o = inv * (d_unit - unit * jnp.mean(d_unit * unit, axis=-1, keepdims=True))
        beta = col_ref[0, :, head : head + 1]
        cum = col_ref[0, :, n + head : n + head + 1]
        tail = col_ref[0, :, 2 * n + head : 2 * n + head + 1]
        q_low, k_low, do_low = queries.astype(LOW), keys.astype(LOW), d_o.astype(LOW)
        exp_cum, exp_tail = jnp.exp(cum), jnp.exp(tail)
        key_tail = keys * exp_tail
        decays, inners, scores, through = [], [], [], []
        for s in range(sz.stacks):
            at = slice(s * sz.stack, (s + 1) * sz.stack)
            decay = decay_of(lower, cum[at], row_ref[0, head : head + 1, at])
            score = mxu(q_low[at], k_low[at], 1, 1) * decay
            inners.append(jnp.where(strict, mxu(k_low[at], k_low[at], 1, 1) * decay, 0.0))
            decays.append(decay)
            scores.append(score)
            through.append(mxu(score, do_low[at], 0, 0))
        held.append(dict(
            kept=kept, q_inv=q_inv, k_inv=k_inv, q_unit=q_unit, keys=keys, values=values,
            d_o=d_o, do_low=do_low, beta=beta, cum=cum, q_low=q_low, k_low=k_low,
            exp_cum=exp_cum, exp_tail=exp_tail, key_tail=key_tail, decays=decays,
            inners=inners, scores=scores, through=through,
            d_right=[None] * sz.chunks, d_q=[None] * sz.chunks, d_k=[None] * sz.chunks,
            d_beta=[None] * sz.chunks, d_cum=[None] * sz.chunks, x=[None] * sz.chunks,
            d_v=[None] * sz.chunks,
        ))
    d_memory = [jnp.zeros((sz.key_dim, sz.value_dim), WIDE) for _ in range(n)]
    for c in reversed(range(sz.chunks)):
        at = slice(c * BLOCK, (c + 1) * BLOCK)
        s, local = c // sz.per_stack, c % sz.per_stack
        in_at = slice(local * BLOCK, (local + 1) * BLOCK)
        for head in range(n):
            m = held[head]
            v_at = slice(head * sz.value_dim, (head + 1) * sz.value_dim)
            memory_low = state_ref[0, head, c]
            grad_low = d_memory[head].astype(LOW)
            d_fresh = m["through"][s][in_at] + mxu(m["key_tail"][at], grad_low)
            d_right = mxu(inv_ref[0, head, s, in_at, in_at], d_fresh, 0, 0)
            d_z = m["beta"][at] * d_right
            lifted = m["exp_cum"][at] * m["d_o"][at]
            sunk = -m["exp_cum"][at] * d_z
            pair = jnp.concatenate([lifted.astype(LOW), sunk.astype(LOW)], axis=0)
            rows = jnp.concatenate([m["q_low"][at], m["k_low"][at]], axis=0)
            last = jnp.exp(m["cum"][(c + 1) * BLOCK - 1 : (c + 1) * BLOCK])
            gend_ref[0, head, c : c + 1, :] = last * jnp.sum(
                d_memory[head] * memory_low.astype(WIDE), axis=0, keepdims=True
            )
            d_tail = mxu(fresh_ref[0, at, v_at], grad_low, 1, 1)
            d_memory[head] = d_memory[head] * last + mxu(rows, pair, 0, 0)
            back = mxu(pair, memory_low, 1, 1)
            both = mxu(rows, memory_low)
            from_keys = m["exp_cum"][at] * both[BLOCK:]
            x = jnp.sum(d_tail * m["key_tail"][at], axis=-1, keepdims=True)
            m["x"][c] = x
            m["d_right"][c] = d_right
            m["d_v"][c] = d_z
            m["d_q"][c] = back[:BLOCK]
            m["d_k"][c] = back[BLOCK:] + d_tail * m["exp_tail"][at]
            m["d_beta"][c] = jnp.sum(
                d_right * (m["values"][at] - from_keys), axis=-1, keepdims=True
            )
            m["d_cum"][c] = (
                jnp.sum(lifted * both[:BLOCK], axis=-1, keepdims=True)
                - jnp.sum(d_z * from_keys, axis=-1, keepdims=True)
                - x
            )
    lane = lax.broadcasted_iota(jnp.int32, (sz.stack, gcol_ref.shape[2]), 1)
    columns = [jnp.zeros((sz.stack, gcol_ref.shape[2]), WIDE) for _ in range(sz.stacks)]
    for head in range(n):
        m = held[head]
        q_at, k_at, v_at, _ = sz.parts(head)
        own = slice(head * sz.value_dim, (head + 1) * sz.value_dim)
        d_q, d_k = [], []
        for s in range(sz.stacks):
            at = slice(s * sz.stack, (s + 1) * sz.stack)
            of = slice(s * sz.per_stack, (s + 1) * sz.per_stack)
            solved = fresh_ref[0, at, own]
            d_right = jnp.concatenate(m["d_right"][of], axis=0)
            d_score = mxu(m["do_low"][at], solved, 1, 1)
            d_inner = -jnp.where(strict, mxu(d_right, solved, 1, 1), 0.0)
            decay, inner, beta = m["decays"][s], m["inners"][s], m["beta"][at]
            d_qk = d_score * decay
            d_kk = d_inner * decay * beta
            by_beta = d_inner * inner
            spread = d_score * m["scores"][s] + by_beta * beta
            d_q.append(jnp.concatenate(m["d_q"][of], axis=0) + mxu(d_qk, m["k_low"][at]))
            d_k.append(
                jnp.concatenate(m["d_k"][of], axis=0)
                + mxu(d_qk, m["q_low"][at], 0, 0)
                + mxu(d_kk, m["k_low"][at], 0, 0)
                + mxu(d_kk, m["k_low"][at])
            )
            grow_ref[0, head : head + 1, at] = jnp.sum(spread, axis=0, keepdims=True)
            d_beta = jnp.concatenate(m["d_beta"][of], axis=0) + jnp.sum(
                by_beta, axis=-1, keepdims=True
            )
            d_cum = jnp.concatenate(m["d_cum"][of], axis=0) + jnp.sum(
                spread, axis=-1, keepdims=True
            )
            x = jnp.concatenate(m["x"][of], axis=0)
            columns[s] = jnp.where(lane == head, d_beta, columns[s])
            columns[s] = jnp.where(lane == n + head, d_cum, columns[s])
            columns[s] = jnp.where(lane == 2 * n + head, x, columns[s])
        d_q = jnp.concatenate(d_q, axis=0)
        d_k = jnp.concatenate(d_k, axis=0)
        d_v = jnp.concatenate(m["d_v"], axis=0)
        q_unit, keys = m["q_unit"], m["keys"]
        d_qs = (sz.key_dim ** -0.5) * m["q_inv"] * (
            d_q - q_unit * jnp.sum(d_q * q_unit, axis=-1, keepdims=True)
        )
        d_ks = m["k_inv"] * (d_k - keys * jnp.sum(d_k * keys, axis=-1, keepdims=True))
        for at, grad, (raw, taps, mixed, sig, _) in zip(
            (q_at, k_at, v_at), (d_qs, d_ks, d_v), m["kept"]
        ):
            d_raw, d_taps = conv_back(grad * silu_back(mixed, sig), raw, taps)
            gp_ref[:, at] = d_raw.astype(LOW)
            for j, member in enumerate(d_taps):
                gtaps_ref[0, j : j + 1, at] = member
    for s in range(sz.stacks):
        gcol_ref[0, s * sz.stack : (s + 1) * sz.stack] = columns[s]
    ga_ref[0] = mxu(xt_ref[...], gp_ref[:, : sz.conv_cols]).astype(LOW).reshape(ga_ref.shape[1:])
    gb_out_ref[0, :, :, :gate_cols] = (
        mxu(xt_ref[...], gp_ref[:, sz.conv_cols :]).astype(LOW).reshape(row_shape + (gate_cols,))
    )
    gin_ref[...] += mxu(gp_ref[...], w_ref[0].reshape(depth, sz.cols), 1, 1)


def out_kernel(mixed_ref, wo_ref, acc_ref):
    @pl.when(pl.program_id(0) == 0)
    def _():
        acc_ref[...] = jnp.zeros_like(acc_ref)

    acc_ref[...] += mxu(mixed_ref[0], out_rows(wo_ref, mixed_ref.shape[2]))


def feed_kernel(rank_ref, order_ref, n_ref, g_ref, w_ref, out_ref, gmid_ref, ga_ref, gb_ref, nf_ref, gf_ref):
    owners, _, width, share = w_ref.shape[1:]

    @pl.when(pl.program_id(0) == 0)
    def _():
        out_ref[...] = jnp.zeros_like(out_ref)
        gmid_ref[...] = jnp.zeros_like(gmid_ref)
        for p in range(owners):
            at = pl.ds(pl.multiple_of(order_ref[p] * share, share), share)
            nf_ref[:, p * share : (p + 1) * share] = n_ref[:, at]
            gf_ref[:, p * share : (p + 1) * share] = g_ref[:, at]

    def weight(which):
        return jnp.concatenate([w_ref[0, i, which] for i in range(owners)], axis=1)

    half = ga_ref.shape[2]
    cut = half - width

    def keep(ref, start, value):
        for p in range(owners):
            ref[0, p, start : start + value.shape[0]] = value[:, p * share : (p + 1) * share]

    rows, grads = n_ref[...], g_ref[...]
    w_gate, w_up, w_down = weight(0), weight(1), weight(2)
    gate = mxu(rows, w_gate, 1, 1)
    up = mxu(rows, w_up, 1, 1)
    sig = jax.nn.sigmoid(gate)
    act = (gate * sig * up).astype(LOW)
    out_ref[...] += mxu(act, w_down)
    d_act = mxu(grads, w_down, 1, 1)
    d_gate = (d_act * up * silu_back(gate, sig)).astype(LOW)
    d_up = (d_act * (gate * sig)).astype(LOW)
    gmid_ref[...] += mxu(d_gate, w_gate) + mxu(d_up, w_up)
    rows, grads = nf_ref[...], gf_ref[...]
    keep(ga_ref, 0, mxu(d_gate, rows, 0, 0).astype(LOW))
    grad_up = mxu(d_up, rows, 0, 0).astype(LOW)
    keep(ga_ref, width, grad_up[:cut])
    keep(gb_ref, 0, grad_up[cut:])
    keep(gb_ref, width - cut, mxu(act, grads, 0, 0).astype(LOW))


def grouped_call(kernel, steps, inputs, outputs, scratch=(), rank=None, group_of=None, flops=1):
    def spec(shape, by_group, buffers, place):
        rest = (0,) * (len(shape) - 1)
        if by_group:
            return pl.BlockSpec(
                (1,) + tuple(shape[1:]),
                lambda s, *r: (place(s, *r),) + rest,
                pipeline_mode=pl.Buffered(buffers),
            )
        return pl.BlockSpec(tuple(shape), lambda s, *r: (0,) + rest)

    def in_step(s, *r):
        return s

    in_place = in_step if group_of is None else lambda s, *r: group_of(s, r[0][0])
    prefetch = () if rank is None else rank
    return pl.pallas_call(
        kernel,
        grid_spec=pltpu.PrefetchScalarGridSpec(
            num_scalar_prefetch=len(prefetch),
            grid=(steps,),
            in_specs=[spec(a.shape, b > 0, b, in_place) for a, b in inputs],
            out_specs=[spec(s, by_group, 2, in_step) for s, _, by_group in outputs],
            scratch_shapes=list(scratch),
        ),
        out_shape=[jax.ShapeDtypeStruct(s, d) for s, d, _ in outputs],
        compiler_params=pltpu.CompilerParams(
            vmem_limit_bytes=VMEM_BYTES, dimension_semantics=("arbitrary",)
        ),
        cost_estimate=pl.CostEstimate(flops=flops, bytes_accessed=1, transcendentals=0),
    )(*prefetch, *[a for a, _ in inputs])


def place_kernel(rank_ref, near_ref, far_ref, layer_ref, tokens_ref):
    from_far = pl.program_id(0) % 2 == 1

    @pl.when(from_far)
    def _():
        layer_ref[0] = far_ref[0, 0]
        tokens_ref[0] = far_ref[0, 1].astype(WIDE)

    @pl.when(jnp.logical_not(from_far))
    def _():
        layer_ref[0] = near_ref[0, 0]
        tokens_ref[0] = near_ref[0, 1].astype(WIDE)


def place_rows(rank, near, far):
    rows, columns = near.shape[2:]
    block = pl.BlockSpec((1, 2, rows, columns), lambda s, r: (s // 2, 0, 0, 0))
    placed = pl.BlockSpec((1, rows, columns), lambda s, r: (s ^ r[0], 0, 0))
    return pl.pallas_call(
        place_kernel,
        grid_spec=pltpu.PrefetchScalarGridSpec(
            num_scalar_prefetch=1, grid=(4,), in_specs=[block, block], out_specs=[placed, placed]
        ),
        out_shape=[
            jax.ShapeDtypeStruct((4, rows, columns), LOW),
            jax.ShapeDtypeStruct((4, rows, columns), WIDE),
        ],
        compiler_params=pltpu.CompilerParams(
            vmem_limit_bytes=VMEM_BYTES, dimension_semantics=("arbitrary",)
        ),
        cost_estimate=pl.CostEstimate(flops=1, bytes_accessed=1, transcendentals=0),
    )(rank, near, far)


def body(
    tokens,
    cotangent,
    live_count,
    norm_first,
    w_query,
    w_key,
    w_value,
    w_out_gate,
    w_beta_decay,
    conv_weight,
    a_log,
    dt_bias,
    out_gain,
    w_out,
    norm_second,
    w_gate,
    w_up,
    w_down,
):
    slot_count, length, model_width = tokens.shape
    total_rows = slot_count * length
    head_count = a_log.shape[0] // lax.axis_size("tensor")
    head_start = lax.axis_index("tensor") * head_count
    conv_local = lax.dynamic_slice_in_dim(conv_weight, head_start, head_count, 1)
    decay_scale = lax.dynamic_slice_in_dim(a_log, head_start, head_count, 0)
    decay_shift = lax.dynamic_slice_in_dim(dt_bias, head_start, head_count, 0)
    shards = (w_query, w_key, w_value, w_out_gate, w_beta_decay, w_out, w_gate, w_up, w_down)
    widened_input, paired_input, out_proj, down_proj = assemble(gather_first(shards), model_width)
    tokens_in = tokens.reshape(total_rows, model_width).astype(jnp.float32)
    scaled_in = unit_rms(tokens_in)
    input_normalized = (scaled_in * norm_first).astype(jnp.bfloat16)
    projected_rows = jnp.dot(input_normalized, widened_input, preferred_element_type=jnp.float32)

    def mix_flat(proj_flat, conv_part, scale_part, shift_part, gain_part):
        return mix_heads(
            proj_flat.reshape(slot_count, length, -1), conv_part, scale_part, shift_part, gain_part
        ).reshape(total_rows, -1)

    mixed_heads, mix_pull = jax.vjp(
        mix_flat, projected_rows, conv_local, decay_scale, decay_shift, out_gain
    )
    mixed_low = mixed_heads.astype(jnp.bfloat16)
    hidden_res = tokens_in + branch_sum(
        jnp.dot(mixed_low, out_proj, preferred_element_type=jnp.float32)
    )
    scaled_mid = unit_rms(hidden_res)
    middle_normalized = (scaled_mid * norm_second).astype(jnp.bfloat16)
    gate_up_product = jnp.dot(middle_normalized, paired_input, preferred_element_type=jnp.float32)
    ff_local = paired_input.shape[1] // 2
    gate_part = gate_up_product[:, :ff_local]
    up_part = gate_up_product[:, ff_local:]
    sigmoid_gate = jax.nn.sigmoid(gate_part)
    silu_gate = gate_part * sigmoid_gate
    activated = (silu_gate * up_part).astype(jnp.bfloat16)
    result_rows = hidden_res + branch_sum(
        jnp.dot(activated, down_proj, preferred_element_type=jnp.float32)
    )
    layer_out = result_rows.astype(jnp.bfloat16).reshape(tokens.shape)
    live_rows = (jnp.arange(slot_count) < live_count[0]).astype(jnp.float32)
    grad_rows = (cotangent.astype(jnp.float32) * live_rows[:, None, None]).reshape(
        total_rows, model_width
    )
    back_wide, back_pair, back_out, back_down = assemble(gather_again(shards), model_width)
    grad_low = grad_rows.astype(jnp.bfloat16)
    grad_down_w = outer_dot(activated, grad_low)
    grad_act = inner_dot(grad_low, back_down)
    grad_gate = grad_act * up_part * sigmoid_gate * (1.0 + gate_part * (1.0 - sigmoid_gate))
    grad_up = grad_act * silu_gate
    grad_pair = jnp.concatenate([grad_gate, grad_up], axis=1).astype(jnp.bfloat16)
    grad_pair_w = outer_dot(middle_normalized, grad_pair)
    grad_mid_part = inner_dot(grad_pair, back_pair)
    gain_mid = jnp.sum(grad_mid_part * scaled_mid, axis=0)
    grad_mid = grad_sum(grad_mid_part)
    grad_hidden = grad_rows + rms_back(hidden_res, grad_mid * norm_second)
    grad_hidden_low = grad_hidden.astype(jnp.bfloat16)
    grad_out_w = outer_dot(mixed_low, grad_hidden_low)
    grad_heads = inner_dot(grad_hidden_low, back_out)
    grad_proj, grad_conv, grad_scale, grad_shift, grad_gain = mix_pull(grad_heads)
    grad_proj_low = grad_proj.astype(jnp.bfloat16)
    grad_wide_w = outer_dot(input_normalized, grad_proj_low)
    grad_in_part = inner_dot(grad_proj_low, back_wide)
    gain_first = jnp.sum(grad_in_part * scaled_in, axis=0)
    grad_in = grad_sum(grad_in_part)
    grad_tokens = grad_hidden + rms_back(tokens_in, grad_in * norm_first)
    query_cols = w_query.shape[1]
    value_cols = w_value.shape[1]
    grad_query = grad_wide_w[:, :query_cols]
    grad_key = grad_wide_w[:, query_cols : 2 * query_cols]
    grad_value = grad_wide_w[:, 2 * query_cols : 2 * query_cols + value_cols]
    grad_gate_out = grad_wide_w[:, 2 * query_cols + value_cols : 2 * query_cols + 2 * value_cols]
    grad_beta_decay = grad_wide_w[:, 2 * query_cols + 2 * value_cols :].reshape(
        model_width, 2, head_count
    )
    reduced = (
        lax.psum_scatter(
            grad_query.astype(jnp.bfloat16), "dp", scatter_dimension=0, tiled=True
        ).astype(jnp.float32),
        lax.psum_scatter(
            grad_key.astype(jnp.bfloat16), "dp", scatter_dimension=0, tiled=True
        ).astype(jnp.float32),
        lax.psum_scatter(
            grad_value.astype(jnp.bfloat16), "dp", scatter_dimension=0, tiled=True
        ).astype(jnp.float32),
        lax.psum_scatter(
            grad_gate_out.astype(jnp.bfloat16), "dp", scatter_dimension=0, tiled=True
        ).astype(jnp.float32),
        lax.psum_scatter(
            grad_beta_decay.astype(jnp.bfloat16), "dp", scatter_dimension=0, tiled=True
        ).astype(jnp.float32),
        lax.psum_scatter(
            grad_out_w.astype(jnp.bfloat16), "dp", scatter_dimension=1, tiled=True
        ).astype(jnp.float32),
        lax.psum_scatter(
            grad_pair_w[:, :ff_local].astype(jnp.bfloat16), "dp", scatter_dimension=0, tiled=True
        ).astype(jnp.float32),
        lax.psum_scatter(
            grad_pair_w[:, ff_local:].astype(jnp.bfloat16), "dp", scatter_dimension=0, tiled=True
        ).astype(jnp.float32),
        lax.psum_scatter(
            grad_down_w.astype(jnp.bfloat16), "dp", scatter_dimension=1, tiled=True
        ).astype(jnp.float32),
    )
    conv_full = lax.dynamic_update_slice_in_dim(
        jnp.zeros_like(conv_weight), grad_conv, head_start, 1
    )
    scale_full = lax.dynamic_update_slice_in_dim(jnp.zeros_like(a_log), grad_scale, head_start, 0)
    shift_full = lax.dynamic_update_slice_in_dim(jnp.zeros_like(dt_bias), grad_shift, head_start, 0)
    small_sums = lax.psum(
        (gain_first, conv_full, scale_full, shift_full, grad_gain, gain_mid), ("dp", "tensor")
    )
    return (
        layer_out,
        grad_tokens.reshape(tokens.shape),
        small_sums[0],
        reduced[0],
        reduced[1],
        reduced[2],
        reduced[3],
        reduced[4],
        small_sums[1],
        small_sums[2],
        small_sums[3],
        small_sums[4],
        reduced[5],
        small_sums[5],
        reduced[6],
        reduced[7],
        reduced[8],
    )


ALL = ("tensor", "dp")


def row_major(array):
    return with_layout_constraint(array, Layout(major_to_minor=tuple(range(array.ndim))))


def gather_all(shard):
    return row_major(lax.all_gather(row_major(shard), ALL, axis=0, tiled=False))


def swap_core(array):
    return lax.ppermute(array, "tensor", [(i, i ^ 1) for i in range(lax.axis_size("tensor"))])


def swap_x(array):
    return lax.ppermute(array, "tensor", [(i, i ^ 2) for i in range(lax.axis_size("tensor"))])


def swap_y(array):
    return lax.ppermute(array, "dp", [(i, i ^ 1) for i in range(lax.axis_size("dp"))])


def swap_z(array, bit):
    return lax.ppermute(array, "dp", [(i, i ^ (2 * bit)) for i in range(lax.axis_size("dp"))])


def shift_z(array, offset):
    count = lax.axis_size("dp")
    return lax.ppermute(array, "dp", [(i, (i + 2 * offset) % count) for i in range(count)])


def sum_everywhere(array):
    array = array + swap_core(array)
    array = array + swap_y(array)
    bit = 1
    while 2 * bit < lax.axis_size("dp"):
        array = array + swap_z(array, bit)
        bit *= 2
    return array + swap_x(array)


def gather_steps(own):
    z_count = lax.axis_size("dp") // 2
    rank, place = lax.axis_index("tensor"), lax.axis_index("dp")
    z_own, y_own = place // 2, place % 2
    array = row_major(jnp.stack([own] + [shift_z(own, -r) for r in range(1, z_count)]))
    array = row_major(jnp.stack([array, swap_y(array)]))
    array = row_major(jnp.stack([array, swap_x(array)]))
    array = row_major(jnp.stack([array, swap_core(array)]))
    array = array.reshape((8 * z_count,) + own.shape)
    t = jnp.arange(4)[:, None] ^ rank
    i = jnp.arange(2 * z_count)[None, :]
    relative = (i // 2 - z_own) % z_count
    index = (((t % 2) * 2 + t // 2) * 2 + ((i % 2) ^ y_own)) * z_count + relative
    return row_major(jnp.take(array, index, axis=0, mode="clip"))


def low_sum(*members):
    total = members[0].astype(WIDE)
    for member in members[1:]:
        total = total + member.astype(WIDE)
    return row_major(total.astype(LOW))


def move_z(array):
    moved = [shift_z(row_major(array[r]), r) for r in range(1, array.shape[0])]
    return (row_major(array[0]),) + tuple(moved)


def sum_z(parts):
    total = parts[0].astype(WIDE)
    for member in parts[1:]:
        total = total + member.astype(WIDE)
    return row_major(total)


def after(array, *others):
    return lax.optimization_barrier((array, others))[0]


def sequence_body(
    tokens,
    cotangent,
    live_count,
    norm_first,
    w_query,
    w_key,
    w_value,
    w_out_gate,
    w_beta_decay,
    conv_weight,
    a_log,
    dt_bias,
    out_gain,
    w_out,
    norm_second,
    w_gate,
    w_up,
    w_down,
):
    groups, owners = lax.axis_size("tensor"), lax.axis_size("dp")
    slot = lax.axis_index("tensor")
    slot_count, length, width = tokens.shape
    tap_count, all_heads, channels = conv_weight.shape
    value_dim = out_gain.shape[0]
    key_dim = (channels - value_dim) // 2
    heads = all_heads // groups
    sz = Sizes(length, heads, key_dim, value_dim)
    share = width // owners
    ff_local = w_gate.shape[1]

    wide_shard = jnp.concatenate([w_query, w_key, w_value, w_out_gate], axis=1)
    wide = gather_all(wide_shard).reshape(groups, owners, share, sz.cols)
    rates_rows = w_beta_decay.reshape(share, 2 * heads).T
    rates_rows = jnp.pad(rates_rows, ((0, -2 * heads % 16), (0, 0)))
    out_w = gather_steps(row_major(jnp.concatenate([w_out, rates_rows], axis=0)))
    small = out_w[:, :, heads * value_dim : heads * value_dim + 2 * heads]
    feed = gather_all(jnp.concatenate([w_gate.T, w_up.T, w_down], axis=0))
    feed = feed.reshape(groups, owners, 3, ff_local, share)

    tokens_in = lax.dynamic_index_in_dim(tokens, slot, 0, keepdims=False).astype(jnp.float32)
    cot_in = lax.dynamic_index_in_dim(cotangent, slot, 0, keepdims=False).astype(jnp.float32)
    grad_rows = cot_in * (slot < live_count[0]).astype(jnp.float32)
    grad_low = grad_rows.astype(LOW)
    scaled_in = unit_rms(tokens_in)
    normed_in = (scaled_in * norm_first).astype(LOW)

    small_cols = jnp.transpose(small, (1, 3, 0, 2)).reshape(width, groups * 2 * heads)
    rates = jnp.dot(normed_in, small_cols, preferred_element_type=jnp.float32)
    rates = rates.reshape(length, groups, 2, heads)
    scale = a_log.reshape(groups, heads)
    shift = dt_bias.reshape(groups, heads)

    up_to = jnp.tril(jnp.ones((BLOCK, BLOCK), jnp.float32))

    def decays(rates, scale, shift):
        beta = jax.nn.sigmoid(rates[:, :, 0])
        gate_log = -jnp.exp(scale) * jax.nn.softplus(rates[:, :, 1] + shift)
        by_block = gate_log.reshape(-1, BLOCK, groups * heads)
        cum = exact_precision("ij,bjn->bin", up_to, by_block)
        tail = cum[:, -1:] - cum
        return (
            beta,
            cum.reshape(length, groups, heads),
            tail.reshape(length, groups, heads),
        )

    (beta, cum, tail), decays_pull = jax.vjp(decays, rates, scale, shift)
    col_form = jnp.moveaxis(jnp.concatenate([beta, cum, tail], axis=2), 1, 0)
    row_form = jnp.moveaxis(cum, 0, 2)
    taps = conv_weight.reshape(tap_count, groups, heads, channels)
    taps = jnp.moveaxis(taps, 1, 0)
    taps = jnp.concatenate(
        [
            taps[..., :key_dim].reshape(groups, tap_count, -1),
            taps[..., key_dim : 2 * key_dim].reshape(groups, tap_count, -1),
            taps[..., 2 * key_dim :].reshape(groups, tap_count, -1),
        ],
        axis=2,
    )
    gain_row = out_gain.reshape(1, value_dim)
    value_cols = heads * value_dim

    proj, mixed, o_rows, fresh, states, inverses = grouped_call(
        functools.partial(forward_kernel, sz),
        groups,
        [(normed_in, 0), (wide, 2), (taps, 2), (col_form, 2), (row_form, 2),
         (gain_row, 0)],
        [
            ((groups, length, sz.cols), jnp.float32, True),
            ((groups, length, value_cols), LOW, True),
            ((groups, length, value_cols), jnp.float32, True),
            ((groups, length, value_cols), LOW, True),
            ((groups, heads, sz.chunks, key_dim, value_dim), LOW, True),
            ((groups, heads, sz.stacks, sz.stack, sz.stack), LOW, True),
        ],
    )
    (branch_mix,) = grouped_call(
        out_kernel,
        groups,
        [(mixed, 2), (out_w, 2)],
        [((length, width), jnp.float32, False)],
    )
    hidden_res = tokens_in + branch_mix
    scaled_mid = unit_rms(hidden_res)
    normed_mid = (scaled_mid * norm_second).astype(LOW)
    z_count = owners // 2
    place = lax.axis_index("dp")
    near_first = jnp.array(
        [((place // 2 + z) % z_count) * 2 + (place % 2) ^ y for y in range(2) for z in range(z_count)]
    )

    rank = slot.astype(jnp.int32).reshape(1)
    half = 3 * ff_local // 2

    def feed_back(core, grads):
        return grouped_call(
            feed_kernel,
            groups // 2,
            [(normed_mid, 0), (grads, 0), (feed, 2)],
            [
                ((length, width), jnp.float32, False),
                ((length, width), jnp.float32, False),
                ((groups // 2, owners, half, share), LOW, True),
                ((groups // 2, owners, half, share), LOW, True),
            ],
            scratch=[pltpu.VMEM((length, width), LOW)] * 2,
            flops=400_000_000_000,
            rank=(rank, near_first.astype(jnp.int32)),
            group_of=lambda s, r: (2 * s + core) ^ r,
        )

    by_feed = (2, 2, z_count, half, share)
    feed_far = feed_back(1, grad_low)
    far_a, far_b = (swap_core(part).reshape(by_feed) for part in feed_far[2:])
    feed_near = feed_back(0, after(grad_low, feed_far[0]))
    near_a, near_b = (part.reshape(by_feed) for part in feed_near[2:])
    feed_x = swap_x(low_sum(near_a[1], far_a[1]))
    feed_y = swap_y(low_sum(near_b[:, 1], far_b[:, 1]))
    layer_own = (hidden_res + (feed_far[0] + feed_near[0])).astype(LOW)
    grad_mid = feed_far[1] + feed_near[1]

    gain_mid = jnp.sum(grad_mid * scaled_mid, axis=0)
    grad_hidden = grad_rows + rms_back(hidden_res, grad_mid * norm_second)
    grad_branch = grad_hidden.astype(LOW)
    def by_distance(rows):
        return jnp.take(rows.reshape(owners, share, -1), near_first, axis=0, mode="clip").reshape(width, -1)

    normed_far = by_distance(normed_in.T)
    branch_far = by_distance(grad_branch.T)

    def mix_back(core, first, count, flops, grad_branch):
        return grouped_call(
            functools.partial(backward_kernel, sz),
            count,
            [(normed_far, 0), (wide, 1), (out_w, 2), (grad_branch, 0), (branch_far, 0),
             (taps, 2), (col_form, 2), (row_form, 2), (gain_row, 0), (proj, 1), (mixed, 2),
             (o_rows, 2), (fresh, 2), (states, 2), (inverses, 2)],
            [
                ((count, owners, share, sz.conv_cols), LOW, True),
                ((count, owners, share, 2 * value_cols), LOW, True),
                ((length, width), jnp.float32, False),
                ((count, length, 128), jnp.float32, True),
                ((count, heads, length), jnp.float32, True),
                ((count, heads, sz.chunks, value_dim), jnp.float32, True),
                ((count, tap_count, sz.conv_cols), jnp.float32, True),
                ((1, value_dim), jnp.float32, False),
            ],
            scratch=[pltpu.VMEM((length, sz.cols), LOW)],
            flops=flops,
            rank=(rank,),
            group_of=lambda s, r: (2 * (s + first) + core) ^ r,
        )

    far = mix_back(1, 0, 2, 400_000_000_000, grad_branch)
    far_conv, far_gate = swap_core(far[0]), swap_core(far[1])
    grad_branch, feed_x, feed_y, _ = lax.optimization_barrier(
        (grad_branch, feed_x, feed_y, far[7])
    )
    feed_xy = swap_y(low_sum(near_a[0, 1], far_a[0, 1], feed_x[1]))
    feed_yx = swap_x(low_sum(near_b[1, 0], far_b[1, 0], feed_y[1]))
    near_x = mix_back(0, 1, 1, 400_000_000_000, grad_branch)
    grad_branch, feed_xy, feed_yx, far_conv, far_gate, _ = lax.optimization_barrier(
        (grad_branch, feed_xy, feed_yx, far_conv, far_gate, near_x[7])
    )
    by_gate = (-1, 2, z_count, share, 2 * value_cols)
    by_conv = (-1, 2, z_count, share, sz.conv_cols)
    far_conv, far_gate = far_conv.reshape(by_conv), far_gate.reshape(by_gate)
    over_conv, over_gate = near_x[0].reshape(by_conv)[0], near_x[1].reshape(by_gate)[0]
    to_conv_x = low_sum(over_conv, far_conv[1])
    to_gate_over = low_sum(over_gate[1], far_gate[1, 1])
    to_feed = jnp.concatenate(
        [
            low_sum(near_a[0, 0], far_a[0, 0], feed_x[0], feed_xy),
            low_sum(near_b[0, 0], far_b[0, 0], feed_y[0], feed_yx),
        ],
        axis=1,
    )
    grad_branch, to_conv_x, to_gate_over, to_feed = lax.optimization_barrier(
        (grad_branch, to_conv_x, to_gate_over, to_feed)
    )
    conv_x, gate_over = swap_x(to_conv_x), swap_y(to_gate_over)
    feed_parts = move_z(to_feed)
    near_own = mix_back(0, 0, 1, 400_000_000_000, grad_branch)
    own_conv, own_gate = near_own[0].reshape(by_conv)[0], near_own[1].reshape(by_gate)[0]
    rest, own_gate, gate_over, feed_next = lax.optimization_barrier(
        (tuple(near_own[2:]), own_gate, gate_over, feed_parts[1])
    )
    feed_parts = feed_parts[:1] + (feed_next,) + feed_parts[2:]
    gate_y = swap_y(low_sum(own_gate[1], far_gate[0, 1]))
    rest, conv_x, gate_y = lax.optimization_barrier((rest, conv_x, gate_y))
    to_conv_xy = low_sum(own_conv[1], far_conv[0, 1], conv_x[1])
    to_gate_yx = low_sum(over_gate[0], far_gate[1, 0], gate_over)
    rest, to_conv_xy, to_gate_yx = lax.optimization_barrier((rest, to_conv_xy, to_gate_yx))
    conv_xy, gate_yx = swap_y(to_conv_xy), swap_x(to_gate_yx)
    near_own = tuple(near_own[:2]) + rest
    grad_in = far[2] + near_x[2] + near_own[2]
    grad_gain = far[7] + near_x[7] + near_own[7]
    near = [jnp.concatenate([first, last]) for first, last in zip(near_own, near_x)]

    def in_order(near_part, far_part):
        both = jnp.stack([near_part, far_part], axis=1)
        both = both.reshape((groups,) + both.shape[2:])
        return jnp.take(both, jnp.arange(groups) ^ slot, axis=0, mode="clip")

    grad_cols, grad_row, grad_end, grad_taps = (
        in_order(near[k][..., : 3 * heads] if k == 3 else near[k],
                 far[k][..., : 3 * heads] if k == 3 else far[k])
        for k in (3, 4, 5, 6)
    )
    grad_cols = jnp.moveaxis(grad_cols, 0, 1)
    grad_beta = grad_cols[:, :, :heads]
    grad_tail = grad_cols[:, :, 2 * heads : 3 * heads]
    grad_cum = grad_cols[:, :, heads : 2 * heads] - jnp.moveaxis(grad_row, 2, 0)
    ends = jnp.moveaxis(jnp.sum(grad_end, axis=-1), 2, 0)
    last_of = (jnp.arange(length) % BLOCK == BLOCK - 1).astype(jnp.float32)
    ends = ends + jnp.sum(grad_tail.reshape(-1, BLOCK, groups, heads), axis=1)
    grad_cum = grad_cum + jnp.repeat(ends, BLOCK, axis=0) * last_of[:, None, None]
    grad_rates, grad_scale, grad_shift = decays_pull(
        (grad_beta, grad_cum, jnp.zeros_like(grad_cum))
    )
    rates_low = grad_rates.reshape(length, -1).astype(LOW)
    rates_low, conv_xy, gate_yx, feed_parts = lax.optimization_barrier(
        (rates_low, conv_xy, gate_yx, feed_parts)
    )
    feed_sum = sum_z(feed_parts)
    grad_small = outer_dot(normed_in, rates_low)
    grad_in = grad_in + inner_dot(rates_low, small_cols)
    gain_first = jnp.sum(grad_in * scaled_in, axis=0)
    grad_own = (grad_hidden + rms_back(tokens_in, grad_in * norm_first)).astype(LOW)

    pieces = (gain_first, grad_taps, grad_scale, grad_shift, grad_gain, gain_mid, grad_small)
    flat = jnp.concatenate([member.reshape(-1) for member in pieces])
    flat = jnp.pad(flat, (0, -flat.shape[0] % 1024)).reshape(-1, 128)
    to_mix = jnp.concatenate(
        [
            low_sum(own_conv[0], far_conv[0, 0], conv_x[0], conv_xy),
            low_sum(own_gate[0], far_gate[0, 0], gate_y, gate_yx),
        ],
        axis=1,
    )
    flat, to_mix, layer_own, grad_own = lax.optimization_barrier(
        (flat, to_mix, layer_own, grad_own)
    )
    mix_parts = move_z(to_mix)
    rows_own = jnp.stack([layer_own, grad_own])
    total = sum_everywhere(flat)
    rows_x, mix_parts, total = lax.optimization_barrier((swap_x(rows_own), mix_parts, total))
    rows_pair = jnp.stack([rows_own, rows_x])
    layer_out, grad_tokens = place_rows(rank, rows_pair, swap_core(rows_pair))
    mix_sum = sum_z(mix_parts)
    conv_sum, gate_sum = mix_sum[:share], mix_sum[share:]
    total = total.reshape(-1)
    sums, start = [], 0
    for member in pieces:
        sums.append(total[start : start + member.size].reshape(member.shape))
        start += member.size
    gain_first, grad_taps, grad_scale, grad_shift, grad_gain, gain_mid, grad_small = sums
    key_cols = heads * key_dim
    grad_conv = jnp.concatenate(
        [
            grad_taps[:, :, :key_cols].reshape(groups, tap_count, heads, key_dim),
            grad_taps[:, :, key_cols : 2 * key_cols].reshape(groups, tap_count, heads, key_dim),
            grad_taps[:, :, 2 * key_cols :].reshape(groups, tap_count, heads, value_dim),
        ],
        axis=3,
    )
    grad_conv = jnp.moveaxis(grad_conv, 0, 1).reshape(conv_weight.shape)
    grad_small = lax.dynamic_slice(
        grad_small,
        (lax.axis_index("dp") * share, slot * 2 * heads),
        (share, 2 * heads),
    ).reshape(w_beta_decay.shape)
    feed_sum = feed_sum.reshape(3, ff_local, share)
    return (
        layer_out,
        grad_tokens,
        gain_first,
        conv_sum[:, :key_cols],
        conv_sum[:, key_cols : 2 * key_cols],
        conv_sum[:, 2 * key_cols :],
        gate_sum[:, :value_cols],
        grad_small,
        grad_conv,
        grad_scale.reshape(-1),
        grad_shift.reshape(-1),
        grad_gain.reshape(-1),
        gate_sum[:, value_cols:].T,
        gain_mid,
        feed_sum[0].T,
        feed_sum[1].T,
        feed_sum[2],
    )


def solution(mesh):
    in_specs = (
        P("dp", None, None),
        P("dp", None, None),
        P("dp"),
        P(),
        P("dp", "tensor"),
        P("dp", "tensor"),
        P("dp", "tensor"),
        P("dp", "tensor"),
        P("dp", None, "tensor"),
        P(),
        P(),
        P(),
        P(),
        P("tensor", "dp"),
        P(),
        P("dp", "tensor"),
        P("dp", "tensor"),
        P("tensor", "dp"),
    )
    out_specs = (
        P("dp", None, None),
        P("dp", None, None),
        P(),
        P("dp", "tensor"),
        P("dp", "tensor"),
        P("dp", "tensor"),
        P("dp", "tensor"),
        P("dp", None, "tensor"),
        P(),
        P(),
        P(),
        P(),
        P("tensor", "dp"),
        P(),
        P("dp", "tensor"),
        P("dp", "tensor"),
        P("tensor", "dp"),
    )
    def plan(*members):
        per_sequence = members[0].shape[0] == mesh.shape["tensor"] == 4
        return (sequence_body if per_sequence else body)(*members)

    return jax.shard_map(plan, mesh=mesh, in_specs=in_specs, out_specs=out_specs, check_vma=False)
```
